256 devices in a mesh: dp: 8 (over x, core), expert: 32 (over y, z).
Axes of the slice: x: 4, y: 4, z: 8, core: 2. Of those that a mesh axis runs over, the one named last changes fastest.
Arguments:
- tokens: bfloat16 [65536, 1280], P(('dp', 'expert')), may hold values from -6 to 6
- norm_gain: float32 [1280], replicated, may hold values from 0.5 to 1.5
- expert_ids: int32 [65536, 1], P(('dp', 'expert')), may hold values from 0 to 31
- priority: int32 [256, 256], P(('dp', 'expert')), may hold values from 0 to 255, each once within a row
- gate_prob: float32 [65536], P(('dp', 'expert')), may hold values from 0.2 to 1
- w_in: bfloat16 [32, 1280, 5120], P('expert', None, 'dp'), may hold values from -0.15625 to 0.15625
- w_out: bfloat16 [32, 5120, 1280], P('expert', 'dp'), may hold values from -0.078125 to 0.078125
- text_emb: float32 [256, 1280], P(('dp', 'expert')), may hold values from -6 to 6
- logit_scale: float32 [1], replicated, may hold values from 10 to 150
Outputs:
- moe_out: bfloat16 [65536, 1280], P(('dp', 'expert'))
- loss: float32 [1], replicated
- grad_image: float32 [256, 1280], P(('dp', 'expert'))
- grad_text: float32 [256, 1280], P(('dp', 'expert'))
The draws below stay inside these ranges and needn't reach their ends.
Inputs may be any that keep to these rules, and one draw needn't show every extreme that they name: `priority`: each row of a group holds a distinct rank. `expert_ids`: every expert is chosen by some patch.
All inputs are finite; a program needn't handle non-finite values.
Results may differ from the reference program's by a relative error of at most 0.0055.
Values may be sent and summed in bfloat16 or wider, within the bound.
No kernel may reach another device: no remote copies, remote signals or barrier semaphores. Data moves between devices by JAX's collectives and lax.ppermute only.
A program may use at most 128 MiB of HBM per device.

```python
import math
import jax
import jax.numpy as jnp
from jax import lax

D = 1280
FF = 5120
PATCHES = 256
EXPERTS = 32
TOK_DEV = 256
CAP = 4
GROUPS = 256
PAIRS = 256
TOKENS = 65536


def shared_parts(key, special):
    normal_part = jax.random.truncated_normal(jax.random.fold_in(key, 101), -4.0, 4.0, (TOKENS, D), jnp.float32)
    noise = 0.5 * normal_part
    common = 0.05 * jax.random.truncated_normal(jax.random.fold_in(key, 104), -4.0, 4.0, (D,), jnp.float32)
    text_noise = 0.03 * jax.random.truncated_normal(jax.random.fold_in(key, 105), -4.0, 4.0, (PAIRS, D), jnp.float32)
    own_dir = 0.05 * jax.random.truncated_normal(jax.random.fold_in(key, 106), -4.0, 4.0, (PAIRS, D), jnp.float32)
    offset = jax.random.randint(jax.random.fold_in(key, 103), (), 0, 32)
    index = jnp.arange(PAIRS, dtype=jnp.int32)
    phase = ((index + offset) % 32)[:, None]
    means = jnp.mean(noise.reshape(PAIRS, PATCHES, D), axis=1)
    strength = 0.3 + 1.2 * index.astype(jnp.float32)[:, None] / PAIRS
    far = jnp.roll(means, PAIRS // 2, axis=0)
    base = strength * means + far + text_noise
    aligned = 3.0 * (own_dir + common[None, :])
    top_sel = (phase == 0).astype(jnp.float32) * special
    text = (1.0 - top_sel) * base
    shift = top_sel * aligned
    tokens = noise + jnp.repeat(shift, PATCHES, axis=0)
    return (tokens, text)


def draw_tokens(key, part):
    tokens, text = shared_parts(key, 0.0)
    return tokens.astype(jnp.bfloat16)


def draw_text_emb(key, part):
    tokens, text = shared_parts(key, 0.0)
    return text


def draw_logit_scale(key, part):
    key = jax.random.fold_in(key, 9)
    value = jnp.exp(jax.random.uniform(key, (1,), jnp.float32, math.log(40.0), math.log(100.0)))
    return value


def levels(stream_key, dims, shards, low, top_value):
    loudness, own = 1.0, jax.random.fold_in(stream_key, 6)
    for dim, shards_of in shards:
        draws = jnp.exp(jax.random.uniform(jax.random.fold_in(own, dim), (shards_of,), jnp.float32, low / len(shards), top_value / len(shards)))
        loudness = loudness * jnp.repeat(draws, dims[dim] // shards_of).reshape([-1 if axis == dim else 1 for axis in range(len(dims))])
    return loudness


def picks_of(key, rows, number_of, top, lift):
    order = jax.random.permutation(jax.random.fold_in(key, 1), number_of)
    favour = order
    for power in range(3):
        favour = favour * favour // number_of
    favour = favour * lift // number_of
    lots = jax.random.randint(jax.random.fold_in(key, 2), (rows, number_of), 0, 4096) + favour
    sure = jax.random.permutation(jax.random.fold_in(key, 3), rows)[jnp.arange(number_of) % rows]
    lots = jnp.where(jnp.arange(rows)[:, None] == sure[None, :], 1 << 14, lots)
    score = lots * number_of + jnp.arange(number_of)
    return lax.top_k(score.astype(jnp.int32), top)[1].astype(jnp.int32)


def scatter_about(key, extent, deviation, limit, split=(), held_as=jnp.bfloat16):
    values = deviation * jax.random.normal(key, extent, jnp.float32)
    if split:
        values = values * levels(key, extent, split, -0.22, 0.18)
    return jnp.clip(values, -limit, limit).astype(held_as)


def setup_inputs(seed: int = 0) -> dict:
    streams_of = jax.random.split(jax.random.key(seed), 10)
    tokens = draw_tokens(jax.random.fold_in(streams_of[9], 71), 0)
    norm_gain = jnp.clip(1.0 + 0.1 * jax.random.normal(streams_of[1], (D,), jnp.float32), 0.5, 1.5)
    expert_ids = picks_of(streams_of[2], TOKENS, EXPERTS, 1, 512)
    priority = jax.vmap(lambda own: jax.random.permutation(own, TOK_DEV))(jax.random.split(streams_of[3], GROUPS)).reshape((GROUPS, TOK_DEV)).astype(jnp.int32)
    gate_prob = jnp.clip(0.2 + 0.8 * jax.random.uniform(streams_of[4], (TOKENS,), jnp.float32) ** levels(streams_of[4], (TOKENS,), ((0, 256),), -0.2, 0.2), 0.2, 1.0)
    w_in = scatter_about(streams_of[5], (EXPERTS, D, FF), D ** -0.5, 0.15625, ((0, 32), (2, 8)))
    w_out = scatter_about(streams_of[6], (EXPERTS, FF, D), FF ** -0.5, 0.078125, ((0, 32), (1, 8)))
    text_emb = draw_text_emb(jax.random.fold_in(streams_of[9], 71), 0)
    logit_scale = draw_logit_scale(jax.random.fold_in(streams_of[9], 71), 0)
    return {"tokens": tokens, "norm_gain": norm_gain, "expert_ids": expert_ids, "priority": priority, "gate_prob": gate_prob, "w_in": w_in, "w_out": w_out, "text_emb": text_emb, "logit_scale": logit_scale}


def layer_norm(block, norm_gain):
    values = block.astype(jnp.float32)
    center = values - lax.optimization_barrier(jnp.mean(values, axis=-1, keepdims=True))
    spread = lax.optimization_barrier(jnp.mean(center * center, axis=-1, keepdims=True))
    return (center * lax.rsqrt(spread + 1e-06) * norm_gain).astype(jnp.bfloat16)

def slot_table(group_ids, ranks):
    same_expert = group_ids[:, None] == group_ids[None, :]
    earlier = ranks[None, :] < ranks[:, None]
    slots = lax.optimization_barrier(jnp.sum((same_expert & earlier).astype(jnp.int32), axis=1))
    target = jnp.where(slots < CAP, group_ids * CAP + slots, -1)
    places = lax.broadcasted_iota(jnp.int32, (EXPERTS * CAP, group_ids.shape[0]), 0)
    return (places == target[None, :]).astype(jnp.bfloat16)

def unit_rows(values):
    radius = jnp.sqrt(lax.optimization_barrier(jnp.sum(values * values, axis=-1, keepdims=True)) + 1e-06)
    return (values / radius, radius)

def back_unit(unit_vals, radius, upstream):
    along = lax.optimization_barrier(jnp.sum(unit_vals * upstream, axis=-1, keepdims=True))
    return (upstream - unit_vals * along) / radius

def reference(tokens, norm_gain, expert_ids, priority, gate_prob, w_in, w_out, text_emb, logit_scale):
    group_count = priority.shape[0]
    starts = jnp.arange(group_count, dtype=jnp.int32)
    flat_ids = expert_ids[:, 0]

    def group_table(index):
        group_ids = lax.dynamic_slice_in_dim(flat_ids, index * TOK_DEV, TOK_DEV, 0)
        return slot_table(group_ids, priority[index])

    def dispatch_group(index):
        block = lax.dynamic_slice_in_dim(tokens, index * TOK_DEV, TOK_DEV, 0)
        normed = layer_norm(block, norm_gain)
        return jnp.dot(group_table(index), normed, preferred_element_type=jnp.float32).astype(jnp.bfloat16)
    buffers = lax.map(dispatch_group, starts)
    by_expert = buffers.reshape(group_count, EXPERTS, CAP, D).transpose(1, 0, 2, 3).reshape(EXPERTS, group_count * CAP, D)

    def run_expert(operands):
        inputs, first, second = operands
        hidden = jax.nn.gelu(jnp.dot(inputs, first, preferred_element_type=jnp.float32)).astype(jnp.bfloat16)
        return jnp.dot(hidden, second, preferred_element_type=jnp.float32).astype(jnp.bfloat16)
    results = lax.map(run_expert, (by_expert, w_in, w_out))
    back = results.reshape(EXPERTS, group_count, CAP, D).transpose(1, 0, 2, 3).reshape(group_count, EXPERTS * CAP, D)

    def combine_group(operands):
        index, returned = operands
        block = lax.dynamic_slice_in_dim(tokens, index * TOK_DEV, TOK_DEV, 0)
        gates = lax.dynamic_slice_in_dim(gate_prob, index * TOK_DEV, TOK_DEV, 0)
        table = group_table(index)
        expert_part = jnp.dot(table.T, returned, preferred_element_type=jnp.float32)
        return (block.astype(jnp.float32) + gates[:, None] * expert_part).astype(jnp.bfloat16)
    moe_out = lax.map(combine_group, (starts, back)).reshape(TOKENS, D)
    pooled = lax.optimization_barrier(jnp.mean(moe_out.astype(jnp.float32).reshape(PAIRS, PATCHES, D), axis=1))
    image_unit, image_radius = unit_rows(pooled)
    text_unit, text_radius = unit_rows(text_emb)
    scale_value = logit_scale[0]
    logits = scale_value * jnp.dot(image_unit, text_unit.T, precision=lax.Precision.HIGHEST)
    row_max = lax.optimization_barrier(jnp.max(logits, axis=1))
    row_lse = row_max + jnp.log(lax.optimization_barrier(jnp.sum(jnp.exp(logits - row_max[:, None]), axis=1)))
    col_max = lax.optimization_barrier(jnp.max(logits, axis=0))
    col_lse = col_max + jnp.log(lax.optimization_barrier(jnp.sum(jnp.exp(logits - col_max[None, :]), axis=0)))
    diagonal = jnp.diagonal(logits)
    loss = (jnp.sum(row_lse) + jnp.sum(col_lse) - 2.0 * jnp.sum(diagonal)) / (2.0 * PAIRS)
    identity = jnp.eye(PAIRS, dtype=jnp.float32)
    grad_logits = (jnp.exp(logits - row_lse[:, None]) + jnp.exp(logits - col_lse[None, :]) - 2.0 * identity) / (2.0 * PAIRS)
    d_image = scale_value * jnp.dot(grad_logits, text_unit, precision=lax.Precision.HIGHEST)
    d_text = scale_value * jnp.dot(grad_logits.T, image_unit, precision=lax.Precision.HIGHEST)
    grad_image = back_unit(image_unit, image_radius, d_image)
    grad_text = back_unit(text_unit, text_radius, d_text)
    return (moe_out, loss.reshape(1), grad_image, grad_text)
```

```python
import jax
import jax.numpy as jnp
from jax import lax
from jax.sharding import PartitionSpec as P

X, CORES, Y, Z = 4, 2, 4, 8
CAP = 4


def along_x(step):
    return "dp", [(x * 2 + c, (x + step) % X * 2 + c) for x in range(X) for c in range(CORES)]


def along_core():
    return "dp", [(i, i ^ 1) for i in range(X * CORES)]


def along_y(step):
    return "expert", [(y * Z + z, (y + step) % Y * Z + z) for y in range(Y) for z in range(Z)]


def along_z(step):
    return "expert", [(y * Z + z, y * Z + (z + step) % Z) for y in range(Y) for z in range(Z)]


def send_to(blocks, along, sign=1):
    return [blocks[0]] + [
        lax.ppermute(blocks[d], *along(sign * d)) for d in range(1, len(blocks))
    ]


def gather_rows(rows, along, count, place):
    got = send_to([rows] * count, along)
    stack = jnp.stack([got[-d % count] for d in range(count)])
    twice = jnp.concatenate([stack, stack])
    ordered = lax.dynamic_slice_in_dim(twice, (count - place) % count, count, 0)
    return ordered


def layer_norm(block, norm_gain):
    values = block.astype(jnp.float32)
    center = values - jnp.mean(values, axis=-1, keepdims=True)
    spread = jnp.mean(center * center, axis=-1, keepdims=True)
    return (center * lax.rsqrt(spread + 1e-06) * norm_gain).astype(jnp.bfloat16)


def slot_table(group_ids, ranks, place_y, place_z):
    same_expert = group_ids[:, None] == group_ids[None, :]
    earlier = ranks[None, :] < ranks[:, None]
    slots = jnp.sum((same_expert & earlier).astype(jnp.int32), axis=1)
    steps = (group_ids // Z - place_y) % Y * Z + (group_ids % Z - place_z) % Z
    target = jnp.where(slots < CAP, steps * CAP + slots, -1)
    places = lax.broadcasted_iota(jnp.int32, (Y * Z * CAP, group_ids.shape[0]), 0)
    return (places == target[None, :]).astype(jnp.bfloat16)


def unit_rows(values):
    radius = jnp.sqrt(jnp.sum(values * values, axis=-1, keepdims=True) + 1e-06)
    return (values / radius, radius)


def back_unit(unit_vals, radius, upstream):
    along = jnp.sum(unit_vals * upstream, axis=-1, keepdims=True)
    return (upstream - unit_vals * along) / radius


def half_expert(inputs, first, second):
    hidden = jax.nn.gelu(jnp.dot(inputs, first, preferred_element_type=jnp.float32))
    return jnp.dot(hidden.astype(jnp.bfloat16), second, preferred_element_type=jnp.float32)


def on_device(
    tokens, norm_gain, expert_ids, priority, gate_prob, w_in, w_out, text_emb, logit_scale
):
    width = tokens.shape[1]
    block = Y * Z * CAP
    expert_place = lax.axis_index("expert")
    place_y, place_z = expert_place // Z, expert_place % Z
    dp_place = lax.axis_index("dp")
    place_x, place_core = dp_place // CORES, dp_place % CORES

    in_own, out_own = w_in[0], w_out[0]
    in_other = lax.ppermute(in_own, *along_core())
    out_other = lax.ppermute(out_own, *along_core())
    text_near = lax.all_gather(text_emb, "expert", axis=0, tiled=True)
    text_all = lax.all_gather(text_near, "dp", axis=0, tiled=True)

    normed = layer_norm(tokens, norm_gain)
    table = slot_table(expert_ids[:, 0], priority[0], place_y, place_z)
    outgoing = jnp.dot(table, normed, preferred_element_type=jnp.float32).astype(jnp.bfloat16)
    outgoing = outgoing.reshape(Y, Z, CAP, width)
    by_z = jnp.stack(send_to([outgoing[:, d] for d in range(Z)], along_z))
    by_y = jnp.stack(send_to([by_z[:, d] for d in range(Y)], along_y))
    incoming = by_y.reshape(block, width)
    rows = jnp.concatenate(send_to([incoming] * X, along_x))

    partial = half_expert(rows, in_own, out_own) + half_expert(rows, in_other, out_other)
    partial = partial.astype(jnp.bfloat16).reshape(X, block, width)
    shares = send_to([partial[d] for d in range(X)], along_x, -1)
    result = sum(share.astype(jnp.float32) for share in shares).astype(jnp.bfloat16)
    result = result.reshape(Y, Z, CAP, width)
    back_y = jnp.stack(send_to([result[d] for d in range(Y)], along_y, -1))
    back_z = send_to([back_y[:, d] for d in range(Z)], along_z, -1)
    returned = jnp.stack(back_z, axis=1).reshape(block, width)
    expert_part = jnp.dot(table.T, returned, preferred_element_type=jnp.float32)
    moe_out = (tokens.astype(jnp.float32) + gate_prob[:, None] * expert_part).astype(jnp.bfloat16)
    pooled = jnp.mean(moe_out.astype(jnp.float32), axis=0, keepdims=True)

    near = gather_rows(pooled, along_z, Z, place_z).reshape(Z, width)
    near = gather_rows(near, along_y, Y, place_y).reshape(Y * Z, width)
    near = gather_rows(near, along_x, X, place_x)
    other = lax.ppermute(near, *along_core())
    pooled_all = jnp.where(
        place_core == 0, jnp.stack([near, other], axis=1), jnp.stack([other, near], axis=1)
    ).reshape(X * CORES * Y * Z, width)
    image_unit, image_radius = unit_rows(pooled_all)
    text_unit, text_radius = unit_rows(text_all)
    pairs = text_all.shape[0]
    me = lax.axis_index(("dp", "expert"))
    scale = logit_scale[0]
    logits = scale * jnp.dot(image_unit, text_unit.T, precision=lax.Precision.HIGHEST)
    row_max = jnp.max(logits, axis=1, keepdims=True)
    col_max = jnp.max(logits, axis=0, keepdims=True)
    row_lse = row_max + jnp.log(jnp.sum(jnp.exp(logits - row_max), axis=1, keepdims=True))
    col_lse = col_max + jnp.log(jnp.sum(jnp.exp(logits - col_max), axis=0, keepdims=True))
    identity = jnp.eye(pairs, dtype=jnp.float32)
    trace = jnp.sum(logits * identity)
    loss = (jnp.sum(row_lse) + jnp.sum(col_lse) - 2.0 * trace) / (2.0 * pairs)
    grad = (jnp.exp(logits - row_lse) + jnp.exp(logits - col_lse) - 2.0 * identity) / (2.0 * pairs)
    grad_row = lax.dynamic_slice_in_dim(grad, me, 1, 0)
    grad_col = lax.dynamic_slice_in_dim(grad, me, 1, 1)
    d_image = scale * jnp.dot(grad_row, text_unit, precision=lax.Precision.HIGHEST)
    d_text = scale * jnp.dot(grad_col.T, image_unit, precision=lax.Precision.HIGHEST)

    def own(values):
        return lax.dynamic_slice_in_dim(values, me, 1, 0)

    grad_image = back_unit(own(image_unit), own(image_radius), d_image)
    grad_text = back_unit(own(text_unit), own(text_radius), d_text)
    return (moe_out, loss.reshape(1), grad_image, grad_text)


def solution(mesh):
    in_specs = (
        P(("dp", "expert"), None),
        P(),
        P(("dp", "expert"), None),
        P(("dp", "expert"), None),
        P(("dp", "expert")),
        P("expert", None, "dp"),
        P("expert", "dp", None),
        P(("dp", "expert"), None),
        P(),
    )
    out_specs = (
        P(("dp", "expert"), None),
        P(),
        P(("dp", "expert"), None),
        P(("dp", "expert"), None),
    )
    return jax.shard_map(
        on_device, mesh=mesh, in_specs=in_specs, out_specs=out_specs, check_vma=False
    )
```

```python
import jax
import jax.numpy as jnp
from jax import lax
from jax.experimental import pallas as pl
from jax.experimental.pallas import tpu as pltpu
from jax.sharding import PartitionSpec as P

X, CORES, Y, Z = 4, 2, 4, 8
CAP = 4
SLOTS = Y * Z * CAP
PAIRS = X * CORES * Y * Z
VMEM = pl.BlockSpec(memory_space=pltpu.VMEM)
SMEM = pl.BlockSpec(memory_space=pltpu.SMEM)


def narrow(values):
    return values.astype(jnp.bfloat16)


def wide(values):
    return values.astype(jnp.float32)


def iota(shape, dim):
    return lax.broadcasted_iota(jnp.int32, shape, dim)


def as_column(row):
    n = row.shape[1]
    same = iota((n, n), 0) == iota((n, n), 1)
    return jnp.sum(jnp.where(same, row, 0.0), axis=1, keepdims=True)


def table_of(target):
    return narrow(wide(iota((SLOTS, target.shape[1]), 0) == target))


def dispatch_kernel(tokens_ref, gain_ref, ids_ref, ranks_ref, out_ref, target_ref):
    ids = ids_ref[...]
    base = wide(ids * 256)
    key = base + wide(ranks_ref[...])
    others = as_column(key)
    earlier = (others >= base) & (others < key)
    slots = jnp.sum(wide(earlier), axis=0, keepdims=True).astype(jnp.int32)
    target = jnp.where(slots < CAP, ids * CAP + slots, -1)
    target_ref[...] = target
    values = wide(tokens_ref[...])
    center = values - jnp.mean(values, axis=-1, keepdims=True)
    spread = jnp.mean(center * center, axis=-1, keepdims=True)
    normed = narrow(center * lax.rsqrt(spread + 1e-06) * gain_ref[...])
    out_ref[...] = narrow(
        jnp.dot(table_of(target), normed, preferred_element_type=jnp.float32)
    )


def dispatch(tokens, gain, ids, ranks):
    rows, width = tokens.shape
    return pl.pallas_call(
        dispatch_kernel,
        out_shape=(
            jax.ShapeDtypeStruct((SLOTS, width), jnp.bfloat16),
            jax.ShapeDtypeStruct((1, rows), jnp.int32),
        ),
        in_specs=[VMEM] * 4,
        out_specs=(VMEM, VMEM),
        name="dispatch",
    )(tokens, gain, ids, ranks)


def combine_kernel(returned_ref, target_ref, gate_ref, tokens_ref, out_ref, pooled_ref):
    expert_part = lax.dot_general(
        table_of(target_ref[...]),
        returned_ref[...],
        (((0,), (0,)), ((), ())),
        preferred_element_type=jnp.float32,
    )
    moe_out = narrow(wide(tokens_ref[...]) + as_column(gate_ref[...]) * expert_part)
    out_ref[...] = moe_out
    pooled = jnp.mean(wide(moe_out), axis=0, keepdims=True)
    pooled_ref[...] = jnp.broadcast_to(pooled, pooled_ref.shape)


def combine(returned, target, gate, tokens):
    rows, width = tokens.shape
    return pl.pallas_call(
        combine_kernel,
        out_shape=(
            jax.ShapeDtypeStruct((rows, width), jnp.bfloat16),
            jax.ShapeDtypeStruct((Y * Z, width), jnp.float32),
        ),
        in_specs=[VMEM] * 4,
        out_specs=(VMEM, VMEM),
        name="combine",
    )(returned, target, gate, tokens)


def contrast_kernel(
    place_ref,
    scale_ref,
    near_ref,
    other_ref,
    text_near_ref,
    text_other_ref,
    loss_ref,
    image_ref,
    dtext_ref,
    image_scr,
    text_scr,
):
    place_x, core, expert = place_ref[0], place_ref[1], place_ref[2]
    me = (place_x * CORES + core) * (Y * Z) + expert
    scale = scale_ref[0]

    def put(scratch, x, c, rows):
        square = jnp.sum(rows * rows, axis=-1, keepdims=True)
        start = pl.multiple_of((x * CORES + c) * (Y * Z), Y * Z)
        scratch[pl.ds(start, Y * Z), :] = rows / jnp.sqrt(square + 1e-06)

    for step in range(X):
        put(image_scr, step, core, near_ref[step])
        put(image_scr, step, 1 - core, other_ref[step])
        put(text_scr, (place_x - step) & (X - 1), core, text_near_ref[step])
        put(text_scr, (place_x - step) & (X - 1), 1 - core, text_other_ref[step])
    image_unit = image_scr[...]
    text_unit = text_scr[...]
    logits = scale * lax.dot_general(
        image_unit,
        text_unit,
        (((1,), (1,)), ((), ())),
        precision=lax.Precision.HIGHEST,
        preferred_element_type=jnp.float32,
    )
    row_max = jnp.max(logits, axis=1, keepdims=True)
    col_max = jnp.max(logits, axis=0, keepdims=True)
    row_lse = row_max + jnp.log(jnp.sum(jnp.exp(logits - row_max), axis=1, keepdims=True))
    col_lse = col_max + jnp.log(jnp.sum(jnp.exp(logits - col_max), axis=0, keepdims=True))
    rows_at, cols_at = iota(logits.shape, 0), iota(logits.shape, 1)
    same = rows_at == cols_at
    trace = jnp.sum(jnp.where(same, logits, 0.0), axis=(0, 1), keepdims=True)
    total = jnp.sum(row_lse, axis=0, keepdims=True) + jnp.sum(col_lse, axis=1, keepdims=True)
    loss_ref[...] = (total - 2.0 * trace) / (2.0 * PAIRS)
    grad = jnp.exp(logits - row_lse) + jnp.exp(logits - col_lse) - 2.0 * wide(same)
    grad = grad / (2.0 * PAIRS)
    own_col = jnp.sum(jnp.where(cols_at == me, grad, 0.0), axis=1, keepdims=True)
    own_row = as_column(jnp.sum(jnp.where(rows_at == me, grad, 0.0), axis=0, keepdims=True))
    d_image = scale * jnp.sum(own_row * text_unit, axis=0, keepdims=True)
    d_text = scale * jnp.sum(own_col * image_unit, axis=0, keepdims=True)

    def back(unit, radius, upstream):
        along = jnp.sum(unit * upstream, axis=-1, keepdims=True)
        return (upstream - unit * along) / radius

    def own(rows):
        radius = jnp.sqrt(jnp.sum(rows * rows, axis=-1, keepdims=True) + 1e-06)
        return rows / radius, radius

    image_ref[...] = back(*own(near_ref[place_x, pl.ds(expert, 1), :]), d_image)
    dtext_ref[...] = back(*own(text_near_ref[0, pl.ds(expert, 1), :]), d_text)


def contrast(places, scale, near, other, text_near, text_other):
    width = near.shape[-1]
    row = jax.ShapeDtypeStruct((1, width), jnp.float32)
    return pl.pallas_call(
        contrast_kernel,
        out_shape=(jax.ShapeDtypeStruct((1, 1), jnp.float32), row, row),
        in_specs=[SMEM, SMEM, VMEM, VMEM, VMEM, VMEM],
        out_specs=(VMEM, VMEM, VMEM),
        scratch_shapes=[pltpu.VMEM((PAIRS, width), jnp.float32)] * 2,
        compiler_params=pltpu.CompilerParams(vmem_limit_bytes=32 * 2**20),
        name="contrast",
    )(places, scale, near, other, text_near, text_other)


HIDDEN_STEP = 128


def expert_kernel(rows_ref, in_own, in_other, out_own, out_other, out_ref):
    first = jnp.concatenate([in_own[...], in_other[...]], axis=1)
    second = jnp.concatenate([out_own[...], out_other[...]], axis=0)
    hidden = jax.nn.gelu(jnp.dot(rows_ref[...], first, preferred_element_type=jnp.float32))
    part = jnp.dot(narrow(hidden), second, preferred_element_type=jnp.float32)

    @pl.when(pl.program_id(0) == 0)
    def _():
        out_ref[...] = part

    @pl.when(pl.program_id(0) > 0)
    def _():
        out_ref[...] += part


def expert_rows(rows, in_own, in_other, out_own, out_other):
    count, width = rows.shape
    hidden = in_own.shape[1]
    whole = pl.BlockSpec((count, width), lambda i: (0, 0))
    first = pl.BlockSpec((width, HIDDEN_STEP), lambda i: (0, i))
    second = pl.BlockSpec((HIDDEN_STEP, width), lambda i: (i, 0))
    return pl.pallas_call(
        expert_kernel,
        grid=(hidden // HIDDEN_STEP,),
        out_shape=jax.ShapeDtypeStruct((count, width), jnp.float32),
        in_specs=[whole, first, first, second, second],
        out_specs=whole,
        compiler_params=pltpu.CompilerParams(vmem_limit_bytes=32 * 2**20),
        cost_estimate=pl.CostEstimate(
            flops=8 * count * width * hidden,
            bytes_accessed=8 * width * hidden + 6 * count * width,
            transcendentals=2 * count * hidden,
        ),
        name="expert",
    )(rows, in_own, in_other, out_own, out_other)


def along_x(step):
    return "dp", [(x * 2 + c, (x + step) % X * 2 + c) for x in range(X) for c in range(CORES)]


def along_core():
    return "dp", [(i, i ^ 1) for i in range(X * CORES)]


def groups_x():
    return [[x * CORES + c for x in range(X)] for c in range(CORES)]


def to_experts(blocks):
    return lax.all_to_all(blocks, "expert", split_axis=0, concat_axis=0, tiled=True)


def on_device(
    tokens, norm_gain, expert_ids, priority, gate_prob, w_in, w_out, text_emb, logit_scale
):
    rows, width = tokens.shape
    half = SLOTS // 2
    dp_place = lax.axis_index("dp")
    places = jnp.stack([dp_place // CORES, dp_place % CORES, lax.axis_index("expert")])

    text_block = to_experts(jnp.broadcast_to(text_emb, (Y * Z, width)))
    weights = (
        w_in[0],
        lax.ppermute(w_in[0], *along_core()),
        w_out[0],
        lax.ppermute(w_out[0], *along_core()),
    )

    outgoing, target = dispatch(
        tokens, norm_gain.reshape(1, width), expert_ids.reshape(1, rows), priority
    )
    text_block, outgoing = lax.optimization_barrier((text_block, outgoing))
    text_x = [text_block] + [lax.ppermute(text_block, *along_x(d)) for d in range(1, X)]
    own_rows = to_experts(outgoing.reshape(Y * Z, CAP, width)).reshape(SLOTS, width)

    text_x, own_rows = lax.optimization_barrier((text_x, own_rows))

    left_rows = lax.ppermute(own_rows, *along_x(1))
    right_rows = lax.ppermute(own_rows, *along_x(-1))
    own_part = expert_rows(own_rows, *weights)
    left_rows, right_rows, own_part = lax.optimization_barrier((left_rows, right_rows, own_part))
    far_rows = jnp.concatenate(
        [
            lax.ppermute(left_rows[:half], *along_x(1)),
            lax.ppermute(right_rows[half:], *along_x(-1)),
        ]
    )
    side_part = expert_rows(jnp.concatenate([left_rows, right_rows]), *weights)
    far_rows, side_part = lax.optimization_barrier((far_rows, side_part))
    far_part = narrow(expert_rows(far_rows, *weights))

    from_right = lax.ppermute(far_part[:half], *along_x(-1))
    from_left = lax.ppermute(far_part[half:], *along_x(1))
    left_sum = jnp.concatenate([side_part[:half] + wide(from_right), side_part[half:SLOTS]])
    right_sum = jnp.concatenate(
        [side_part[SLOTS : SLOTS + half], side_part[SLOTS + half :] + wide(from_left)]
    )
    left_sum = lax.ppermute(narrow(left_sum), *along_x(-1))
    right_sum = lax.ppermute(narrow(right_sum), *along_x(1))
    result = narrow(own_part + wide(left_sum) + wide(right_sum))

    text_near, result = lax.optimization_barrier((jnp.stack(text_x), result))
    text_other = lax.ppermute(text_near, *along_core())
    returned = to_experts(result.reshape(Y * Z, CAP, width)).reshape(SLOTS, width)
    moe_out, pooled = combine(returned, target, gate_prob.reshape(1, rows), tokens)

    near = to_experts(pooled)
    near = lax.all_to_all(
        jnp.broadcast_to(near, (X,) + near.shape),
        "dp",
        split_axis=0,
        concat_axis=0,
        tiled=True,
        axis_index_groups=groups_x(),
    )
    other = lax.ppermute(near, *along_core())
    loss, grad_image, grad_text = contrast(
        places, logit_scale, near, other, text_near, text_other
    )
    return (moe_out, loss.reshape(1), grad_image, grad_text)


def solution(mesh):
    in_specs = (
        P(("dp", "expert"), None),
        P(),
        P(("dp", "expert"), None),
        P(("dp", "expert"), None),
        P(("dp", "expert")),
        P("expert", None, "dp"),
        P("expert", "dp", None),
        P(("dp", "expert"), None),
        P(),
    )
    out_specs = (
        P(("dp", "expert"), None),
        P(),
        P(("dp", "expert"), None),
        P(("dp", "expert"), None),
    )
    return jax.shard_map(
        on_device, mesh=mesh, in_specs=in_specs, out_specs=out_specs, check_vma=False
    )
```

```python
import jax
import jax.numpy as jnp
from jax import lax
from jax.experimental import pallas as pl
from jax.experimental.pallas import tpu as pltpu
from jax.sharding import PartitionSpec as P

X, CORES, Y, Z = 4, 2, 4, 8
CAP = 4
ROWS, PARTS = 8, 3
LANES, WIDTH = 128, 1280
SLOTS = Y * Z * CAP
PAIRS = X * CORES * Y * Z
VMEM = pl.BlockSpec(memory_space=pltpu.VMEM)
SMEM = pl.BlockSpec(memory_space=pltpu.SMEM)


def narrow(values):
    return values.astype(jnp.bfloat16)


def wide(values):
    return values.astype(jnp.float32)


def iota(shape, dim):
    return lax.broadcasted_iota(jnp.int32, shape, dim)


def as_column(row):
    n = row.shape[1]
    same = iota((n, n), 0) == iota((n, n), 1)
    return jnp.sum(jnp.where(same, row, 0.0), axis=1, keepdims=True)


def table_of(target):
    return narrow(wide(iota((SLOTS, target.shape[1]), 0) == target))


def dispatch_kernel(tokens_ref, gain_ref, ids_ref, ranks_ref, text_ref, out_ref, target_ref):
    ids = ids_ref[...]
    base = wide(ids * 256)
    key = base + wide(ranks_ref[...])
    others = as_column(key)
    earlier = (others >= base) & (others < key)
    slots = jnp.sum(wide(earlier), axis=0, keepdims=True).astype(jnp.int32)
    kept = slots < CAP
    target_ref[...] = jnp.where(kept, ids * CAP + slots, -1)
    values = wide(tokens_ref[...])
    center = values - jnp.mean(values, axis=-1, keepdims=True)
    spread = jnp.mean(center * center, axis=-1, keepdims=True)
    gain = jnp.concatenate([gain_ref[i : i + 1, :] for i in range(gain_ref.shape[0])], axis=1)
    normed = narrow(center * lax.rsqrt(spread + 1e-06) * gain)
    table = narrow(wide(iota((Y * Z * ROWS, ids.shape[1]), 0) == jnp.where(kept, ids * ROWS + slots, -1)))
    picked = jnp.dot(table, normed, preferred_element_type=jnp.float32)
    part = iota(picked.shape, 0) & (ROWS - 1)
    rest = text_ref[...]
    for index in range(PARTS):
        piece = wide(narrow(rest))
        rest = rest - piece
        picked = jnp.where(part == CAP + index, piece, picked)
    out_ref[...] = narrow(picked)


def dispatch(tokens, gain, ids, ranks, text):
    rows, width = tokens.shape
    return pl.pallas_call(
        dispatch_kernel,
        out_shape=(
            jax.ShapeDtypeStruct((Y * Z * ROWS, width), jnp.bfloat16),
            jax.ShapeDtypeStruct((1, rows), jnp.int32),
        ),
        in_specs=[VMEM] * 5,
        out_specs=(VMEM, VMEM),
        compiler_params=pltpu.CompilerParams(vmem_limit_bytes=32 * 2**20),
        name="dispatch",
    )(tokens, gain, ids, ranks, text)


def unpack_kernel(blocks_ref, rows_ref, text_ref):
    blocks = blocks_ref[...]
    count = blocks.shape[0]
    row, col = iota((SLOTS, count), 0), iota((SLOTS, count), 1)
    pick = narrow(wide(col == (row >> 2) * ROWS + (row & (CAP - 1))))
    rows_ref[...] = narrow(jnp.dot(pick, blocks, preferred_element_type=jnp.float32))
    row, col = iota((Y * Z, count), 0), iota((Y * Z, count), 1)
    part = col - row * ROWS
    pick = narrow(wide((part >= CAP) & (part < CAP + PARTS)))
    text_ref[...] = jnp.dot(pick, blocks, preferred_element_type=jnp.float32)


def unpack(blocks):
    width = blocks.shape[1]
    return pl.pallas_call(
        unpack_kernel,
        out_shape=(
            jax.ShapeDtypeStruct((SLOTS, width), jnp.bfloat16),
            jax.ShapeDtypeStruct((Y * Z, width), jnp.float32),
        ),
        in_specs=[VMEM],
        out_specs=(VMEM, VMEM),
        name="unpack",
    )(blocks)


def combine_kernel(returned_ref, target_ref, gate_ref, tokens_ref, out_ref, pooled_ref):
    expert_part = lax.dot_general(
        table_of(target_ref[...]),
        returned_ref[...],
        (((0,), (0,)), ((), ())),
        preferred_element_type=jnp.float32,
    )
    moe_out = narrow(wide(tokens_ref[...]) + as_column(gate_ref[...]) * expert_part)
    out_ref[...] = moe_out
    pooled = jnp.mean(wide(moe_out), axis=0, keepdims=True)
    pieces = pooled.shape[1] // LANES
    for index in range(pieces):
        piece = pooled[:, index * LANES : (index + 1) * LANES]
        pooled_ref[pl.ds(index, Y * Z, stride=pieces), :] = jnp.broadcast_to(piece, (Y * Z, LANES))


def combine(returned, target, gate, tokens):
    rows, width = tokens.shape
    return pl.pallas_call(
        combine_kernel,
        out_shape=(
            jax.ShapeDtypeStruct((rows, width), jnp.bfloat16),
            jax.ShapeDtypeStruct((Y * Z * width // LANES, LANES), jnp.float32),
        ),
        in_specs=[VMEM] * 4,
        out_specs=(VMEM, VMEM),
        name="combine",
    )(returned, target, gate, tokens)


def full_rows(ref):
    pieces = WIDTH // LANES
    count = ref.shape[0] // pieces
    return jnp.concatenate(
        [ref[pl.ds(i, count, stride=pieces), :] for i in range(pieces)], axis=1
    )


def contrast_kernel(place_ref, scale_ref, *refs):
    images, texts = (refs[:5], refs[5:10]), (refs[10:14], refs[14:18])
    loss_ref, image_ref, dtext_ref, image_scr, text_scr = refs[18:]
    place_x, core, expert = place_ref[0], place_ref[1], place_ref[2]
    me = (place_x * CORES + core) * (Y * Z) + expert
    scale = scale_ref[0]

    def put(scratch, x, c, first, rows):
        square = jnp.sum(rows * rows, axis=-1, keepdims=True)
        start = pl.multiple_of((x & (X - 1)) * (CORES * Y * Z) + c * (Y * Z) + first, 8)
        scratch[pl.ds(start, rows.shape[0]), :] = rows / jnp.sqrt(square + 1e-06)

    half = Y * Z // 2
    for side in range(CORES):
        c = core + side - 2 * core * side
        for ref, step, first in zip(images[side], (0, 3, 1, 2, 2), (0, 0, 0, 0, half)):
            put(image_scr, place_x + step, c, first, full_rows(ref))
        for ref, step in zip(texts[side], (0, 3, 2, 1)):
            put(text_scr, place_x + step, c, 0, ref[...])
    image_unit = image_scr[...]
    text_unit = text_scr[...]
    logits = scale * lax.dot_general(
        image_unit,
        text_unit,
        (((1,), (1,)), ((), ())),
        precision=lax.Precision.HIGHEST,
        preferred_element_type=jnp.float32,
    )
    row_max = jnp.max(logits, axis=1, keepdims=True)
    col_max = jnp.max(logits, axis=0, keepdims=True)
    row_lse = row_max + jnp.log(jnp.sum(jnp.exp(logits - row_max), axis=1, keepdims=True))
    col_lse = col_max + jnp.log(jnp.sum(jnp.exp(logits - col_max), axis=0, keepdims=True))
    rows_at, cols_at = iota(logits.shape, 0), iota(logits.shape, 1)
    same = rows_at == cols_at
    trace = jnp.sum(jnp.where(same, logits, 0.0), axis=(0, 1), keepdims=True)
    total = jnp.sum(row_lse, axis=0, keepdims=True) + jnp.sum(col_lse, axis=1, keepdims=True)
    loss_ref[...] = (total - 2.0 * trace) / (2.0 * PAIRS)
    grad = jnp.exp(logits - row_lse) + jnp.exp(logits - col_lse) - 2.0 * wide(same)
    grad = grad / (2.0 * PAIRS)
    own_col = jnp.sum(jnp.where(cols_at == me, grad, 0.0), axis=1, keepdims=True)
    own_row = as_column(jnp.sum(jnp.where(rows_at == me, grad, 0.0), axis=0, keepdims=True))
    d_image = scale * jnp.sum(own_row * text_unit, axis=0, keepdims=True)
    d_text = scale * jnp.sum(own_col * image_unit, axis=0, keepdims=True)

    def back(unit, radius, upstream):
        along = jnp.sum(unit * upstream, axis=-1, keepdims=True)
        return (upstream - unit * along) / radius

    def own(rows):
        radius = jnp.sqrt(jnp.sum(rows * rows, axis=-1, keepdims=True) + 1e-06)
        return rows / radius, radius

    pieces = WIDTH // LANES
    own_image = jnp.concatenate(
        [images[0][0][pl.ds(expert * pieces + i, 1), :] for i in range(pieces)], axis=1
    )
    image_ref[...] = back(*own(own_image), d_image)
    dtext_ref[...] = back(*own(texts[0][0][pl.ds(expert, 1), :]), d_text)


def contrast(places, scale, images, other_images, texts, other_texts):
    row = jax.ShapeDtypeStruct((1, WIDTH), jnp.float32)
    return pl.pallas_call(
        contrast_kernel,
        out_shape=(jax.ShapeDtypeStruct((1, 1), jnp.float32), row, row),
        in_specs=[SMEM, SMEM] + [VMEM] * 18,
        out_specs=(VMEM, VMEM, VMEM),
        scratch_shapes=[pltpu.VMEM((PAIRS, WIDTH), jnp.float32)] * 2,
        compiler_params=pltpu.CompilerParams(vmem_limit_bytes=32 * 2**20),
        name="contrast",
    )(places, scale, *images, *other_images, *texts, *other_texts)


def expert_kernel(rows_ref, in_own, in_other, out_own, out_other, out_ref, hidden_scr):
    rows = rows_ref[...]
    share = in_own.shape[1]
    tile = 2 * LANES
    whole = share // tile * tile
    cuts = [slice(i, i + tile) for i in range(0, whole, tile)]

    def hidden_of(first):
        hidden = jax.nn.gelu(jnp.dot(rows, first, preferred_element_type=jnp.float32))
        return narrow(hidden)

    for cut in cuts:
        hidden_scr[:, cut] = hidden_of(in_own[:, cut])
        hidden_scr[:, share + cut.start : share + cut.stop] = hidden_of(in_other[:, cut])
    last = hidden_of(jnp.concatenate([in_own[:, whole:], in_other[:, whole:]], axis=1))
    hidden_scr[:, whole:share] = last[:, : share - whole]
    hidden_scr[:, share + whole :] = last[:, share - whole :]
    hidden = hidden_scr[...]
    for i in range(0, out_ref.shape[1], tile):
        cut = slice(i, i + tile)
        second = jnp.concatenate([out_own[:, cut], out_other[:, cut]], axis=0)
        out_ref[:, cut] = jnp.dot(hidden, second, preferred_element_type=jnp.float32)


def expert_rows(rows, in_own, in_other, out_own, out_other):
    count, width = rows.shape
    hidden = in_own.shape[1]
    return pl.pallas_call(
        expert_kernel,
        out_shape=jax.ShapeDtypeStruct((count, width), jnp.float32),
        in_specs=[VMEM] * 5,
        out_specs=VMEM,
        scratch_shapes=[pltpu.VMEM((count, 2 * hidden), jnp.bfloat16)],
        compiler_params=pltpu.CompilerParams(vmem_limit_bytes=32 * 2**20),
        cost_estimate=pl.CostEstimate(
            flops=8 * count * width * hidden,
            bytes_accessed=8 * width * hidden + 6 * count * width,
            transcendentals=2 * count * hidden,
        ),
        name="expert",
    )(rows, in_own, in_other, out_own, out_other)


def along_x(step):
    return "dp", [(x * 2 + c, (x + step) % X * 2 + c) for x in range(X) for c in range(CORES)]


def along_core():
    return "dp", [(i, i ^ 1) for i in range(X * CORES)]


def to_experts(blocks):
    return lax.all_to_all(blocks, "expert", split_axis=0, concat_axis=0, tiled=True)


def on_device(
    tokens, norm_gain, expert_ids, priority, gate_prob, w_in, w_out, text_emb, logit_scale
):
    rows, width = tokens.shape
    half = SLOTS // 2
    dp_place = lax.axis_index("dp")
    places = jnp.stack([dp_place // CORES, dp_place % CORES, lax.axis_index("expert")])

    weights = (
        w_in[0],
        lax.ppermute(w_in[0], *along_core()),
        w_out[0],
        lax.ppermute(w_out[0], *along_core()),
    )

    outgoing, target = dispatch(
        tokens,
        norm_gain.reshape(width // LANES, LANES),
        expert_ids.reshape(1, rows),
        priority,
        text_emb,
    )
    incoming = to_experts(outgoing.reshape(Y * Z, ROWS, width))
    own_rows, text_block = unpack(incoming.reshape(Y * Z * ROWS, width))

    left_rows = lax.ppermute(own_rows, *along_x(1))
    right_rows = lax.ppermute(own_rows, *along_x(-1))
    own_part = expert_rows(own_rows, *weights)
    left_rows, right_rows, own_part = lax.optimization_barrier((left_rows, right_rows, own_part))
    far_rows = jnp.concatenate(
        [
            lax.ppermute(left_rows[:half], *along_x(1)),
            lax.ppermute(right_rows[half:], *along_x(-1)),
        ]
    )
    side_part = expert_rows(jnp.concatenate([left_rows, right_rows]), *weights)
    far_rows, side_part = lax.optimization_barrier((far_rows, side_part))
    far_part = narrow(expert_rows(far_rows, *weights))

    from_right = lax.ppermute(far_part[:half], *along_x(-1))
    from_left = lax.ppermute(far_part[half:], *along_x(1))
    left_sum = jnp.concatenate([side_part[:half] + wide(from_right), side_part[half:SLOTS]])
    right_sum = jnp.concatenate(
        [side_part[SLOTS : SLOTS + half], side_part[SLOTS + half :] + wide(from_left)]
    )
    left_sum = lax.ppermute(narrow(left_sum), *along_x(-1))
    right_sum = lax.ppermute(narrow(right_sum), *along_x(1))
    result = narrow(own_part + wide(left_sum) + wide(right_sum))

    text_block, result = lax.optimization_barrier((text_block, result))
    texts = [text_block] + [lax.ppermute(text_block, *along_x(d)) for d in range(1, X)]
    returned = to_experts(result.reshape(Y * Z, CAP, width)).reshape(SLOTS, width)
    texts, returned = lax.optimization_barrier((texts, returned))
    moe_out, pooled = combine(returned, target, gate_prob.reshape(1, rows), tokens)

    near = to_experts(pooled.reshape(Y * Z, 1, width)).reshape(pooled.shape)
    half = near.shape[0] // 2
    left = lax.ppermute(near, *along_x(1))
    right = lax.ppermute(near, *along_x(-1))
    far = [lax.ppermute(left[:half], *along_x(1)), lax.ppermute(right[half:], *along_x(-1))]
    images = [near, left, right] + far
    loss, grad_image, grad_text = contrast(
        places,
        logit_scale,
        images,
        [lax.ppermute(block, *along_core()) for block in images],
        texts,
        [lax.ppermute(block, *along_core()) for block in texts],
    )
    return (moe_out, loss.reshape(1), grad_image, grad_text)


def solution(mesh):
    in_specs = (
        P(("dp", "expert"), None),
        P(),
        P(("dp", "expert"), None),
        P(("dp", "expert"), None),
        P(("dp", "expert")),
        P("expert", None, "dp"),
        P("expert", "dp", None),
        P(("dp", "expert"), None),
        P(),
    )
    out_specs = (
        P(("dp", "expert"), None),
        P(),
        P(("dp", "expert"), None),
        P(("dp", "expert"), None),
    )
    return jax.shard_map(
        on_device, mesh=mesh, in_specs=in_specs, out_specs=out_specs, check_vma=False
    )
```

```python
import jax
import jax.numpy as jnp
from jax import lax
from jax.experimental import pallas as pl
from jax.experimental.pallas import tpu as pltpu
from jax.sharding import PartitionSpec as P

X, CORES, Y, Z = 4, 2, 4, 8
CAP = 4
LANES, WIDTH = 128, 1280
SLOTS = Y * Z * CAP
PAIRS = X * CORES * Y * Z
VMEM = pl.BlockSpec(memory_space=pltpu.VMEM)
HBM = pl.BlockSpec(memory_space=pltpu.HBM)
SMEM = pl.BlockSpec(memory_space=pltpu.SMEM)


def narrow(values):
    return values.astype(jnp.bfloat16)


def wide(values):
    return values.astype(jnp.float32)


def iota(shape, dim):
    return lax.broadcasted_iota(jnp.int32, shape, dim)


def as_column(row):
    n = row.shape[1]
    same = iota((n, n), 0) == iota((n, n), 1)
    return jnp.sum(jnp.where(same, row, 0.0), axis=1, keepdims=True)


def table_of(target):
    return narrow(wide(iota((SLOTS, target.shape[1]), 0) == target))


def fetch(pairs, sems):
    copies = [
        pltpu.make_async_copy(source, target, sems.at[i]) for i, (source, target) in enumerate(pairs)
    ]
    for copy in copies:
        copy.start()
    for copy in copies:
        copy.wait()


def dispatch_kernel(tokens_hbm, gain_hbm, ids_hbm, ranks_hbm, out_ref, target_ref, *scratch):
    tokens_ref, gain_ref, ids_ref, ranks_ref, sems = scratch
    sources = (tokens_hbm, gain_hbm, ids_hbm, ranks_hbm)
    fetch(list(zip(sources, (tokens_ref, gain_ref, ids_ref, ranks_ref))), sems)
    ids = ids_ref[...]
    base = wide(ids * 256)
    key = base + wide(ranks_ref[...])
    others = as_column(key)
    earlier = (others >= base) & (others < key)
    slots = jnp.sum(wide(earlier), axis=0, keepdims=True).astype(jnp.int32)
    target = jnp.where(slots < CAP, ids * CAP + slots, -1)
    target_ref[...] = target
    values = wide(tokens_ref[...])
    center = values - jnp.mean(values, axis=-1, keepdims=True)
    spread = jnp.mean(center * center, axis=-1, keepdims=True)
    gain = jnp.concatenate([gain_ref[i : i + 1, :] for i in range(gain_ref.shape[0])], axis=1)
    normed = narrow(center * lax.rsqrt(spread + 1e-06) * gain)
    out_ref[...] = narrow(
        jnp.dot(table_of(target), normed, preferred_element_type=jnp.float32)
    )


def dispatch(tokens, gain, ids, ranks):
    rows, width = tokens.shape
    inputs = (tokens, gain, ids, ranks)
    return pl.pallas_call(
        dispatch_kernel,
        out_shape=(
            jax.ShapeDtypeStruct((SLOTS, width), jnp.bfloat16),
            jax.ShapeDtypeStruct((1, rows), jnp.int32),
        ),
        in_specs=[HBM] * 4,
        out_specs=(VMEM, VMEM),
        scratch_shapes=[pltpu.VMEM(x.shape, x.dtype) for x in inputs]
        + [pltpu.SemaphoreType.DMA((len(inputs),))],
        compiler_params=pltpu.CompilerParams(vmem_limit_bytes=64 * 2**20),
        name="dispatch",
    )(*inputs)


def combine_kernel(returned_ref, target_ref, gate_ref, tokens_ref, out_ref, pooled_ref):
    expert_part = lax.dot_general(
        table_of(target_ref[...]),
        returned_ref[...],
        (((0,), (0,)), ((), ())),
        preferred_element_type=jnp.float32,
    )
    moe_out = narrow(wide(tokens_ref[...]) + as_column(gate_ref[...]) * expert_part)
    out_ref[...] = moe_out
    pooled = jnp.mean(wide(moe_out), axis=0, keepdims=True)
    pieces = pooled.shape[1] // LANES
    for index in range(pieces):
        piece = pooled[:, index * LANES : (index + 1) * LANES]
        pooled_ref[pl.ds(index, Y * Z, stride=pieces), :] = jnp.broadcast_to(piece, (Y * Z, LANES))


def combine(returned, target, gate, tokens):
    rows, width = tokens.shape
    return pl.pallas_call(
        combine_kernel,
        out_shape=(
            jax.ShapeDtypeStruct((rows, width), jnp.bfloat16),
            jax.ShapeDtypeStruct((Y * Z * width // LANES, LANES), jnp.float32),
        ),
        in_specs=[VMEM] * 4,
        out_specs=(VMEM, VMEM),
        name="combine",
    )(returned, target, gate, tokens)


def full_rows(ref):
    pieces = WIDTH // LANES
    count = ref.shape[0] // pieces
    return jnp.concatenate(
        [ref[pl.ds(i, count, stride=pieces), :] for i in range(pieces)], axis=1
    )


def contrast_kernel(place_ref, scale_ref, *refs):
    images, texts = (refs[:5], refs[5:10]), (refs[10:14], refs[14:18])
    loss_ref, image_ref, dtext_ref, image_scr, text_scr = refs[18:]
    place_x, core, expert = place_ref[0], place_ref[1], place_ref[2]
    me = (place_x * CORES + core) * (Y * Z) + expert
    scale = scale_ref[0]

    def put(scratch, x, c, first, rows):
        square = jnp.sum(rows * rows, axis=-1, keepdims=True)
        start = pl.multiple_of((x & (X - 1)) * (CORES * Y * Z) + c * (Y * Z) + first, 8)
        scratch[pl.ds(start, rows.shape[0]), :] = rows / jnp.sqrt(square + 1e-06)

    half = Y * Z // 2
    for side in range(CORES):
        c = core + side - 2 * core * side
        for ref, step, first in zip(images[side], (0, 3, 1, 2, 2), (0, 0, 0, 0, half)):
            put(image_scr, place_x + step, c, first, full_rows(ref))
        for ref, step in zip(texts[side], (0, 3, 2, 1)):
            put(text_scr, place_x + step, c, 0, full_rows(ref))
    image_unit = image_scr[...]
    text_unit = text_scr[...]
    logits = scale * lax.dot_general(
        image_unit,
        text_unit,
        (((1,), (1,)), ((), ())),
        precision=lax.Precision.HIGHEST,
        preferred_element_type=jnp.float32,
    )
    row_max = jnp.max(logits, axis=1, keepdims=True)
    col_max = jnp.max(logits, axis=0, keepdims=True)
    row_lse = row_max + jnp.log(jnp.sum(jnp.exp(logits - row_max), axis=1, keepdims=True))
    col_lse = col_max + jnp.log(jnp.sum(jnp.exp(logits - col_max), axis=0, keepdims=True))
    rows_at, cols_at = iota(logits.shape, 0), iota(logits.shape, 1)
    same = rows_at == cols_at
    trace = jnp.sum(jnp.where(same, logits, 0.0), axis=(0, 1), keepdims=True)
    total = jnp.sum(row_lse, axis=0, keepdims=True) + jnp.sum(col_lse, axis=1, keepdims=True)
    loss_ref[...] = (total - 2.0 * trace) / (2.0 * PAIRS)
    grad = jnp.exp(logits - row_lse) + jnp.exp(logits - col_lse) - 2.0 * wide(same)
    grad = grad / (2.0 * PAIRS)
    own_col = jnp.sum(jnp.where(cols_at == me, grad, 0.0), axis=1, keepdims=True)
    own_row = as_column(jnp.sum(jnp.where(rows_at == me, grad, 0.0), axis=0, keepdims=True))
    d_image = scale * jnp.sum(own_row * text_unit, axis=0, keepdims=True)
    d_text = scale * jnp.sum(own_col * image_unit, axis=0, keepdims=True)

    def back(unit, radius, upstream):
        along = jnp.sum(unit * upstream, axis=-1, keepdims=True)
        return (upstream - unit * along) / radius

    def own(rows):
        radius = jnp.sqrt(jnp.sum(rows * rows, axis=-1, keepdims=True) + 1e-06)
        return rows / radius, radius

    def own_row(ref):
        pieces = WIDTH // LANES
        return jnp.concatenate(
            [ref[pl.ds(expert * pieces + i, 1), :] for i in range(pieces)], axis=1
        )

    image_ref[...] = back(*own(own_row(images[0][0])), d_image)
    dtext_ref[...] = back(*own(own_row(texts[0][0])), d_text)


def contrast(places, scale, images, other_images, texts, other_texts):
    row = jax.ShapeDtypeStruct((1, WIDTH), jnp.float32)
    return pl.pallas_call(
        contrast_kernel,
        out_shape=(jax.ShapeDtypeStruct((1, 1), jnp.float32), row, row),
        in_specs=[SMEM, SMEM] + [VMEM] * 18,
        out_specs=(VMEM, VMEM, VMEM),
        scratch_shapes=[pltpu.VMEM((PAIRS, WIDTH), jnp.float32)] * 2,
        compiler_params=pltpu.CompilerParams(vmem_limit_bytes=32 * 2**20),
        name="contrast",
    )(places, scale, *images, *other_images, *texts, *other_texts)


def expert_kernel(rows_ref, in_own, in_other, out_own, out_other, out_ref, hidden_scr):
    rows = rows_ref[...]
    share = in_own.shape[1]
    tile = 2 * LANES
    whole = share // tile * tile
    cuts = [slice(i, i + tile) for i in range(0, whole, tile)]

    def hidden_of(first):
        hidden = jax.nn.gelu(jnp.dot(rows, first, preferred_element_type=jnp.float32))
        return narrow(hidden)

    for cut in cuts:
        hidden_scr[:, cut] = hidden_of(in_own[:, cut])
        hidden_scr[:, share + cut.start : share + cut.stop] = hidden_of(in_other[:, cut])
    last = hidden_of(jnp.concatenate([in_own[:, whole:], in_other[:, whole:]], axis=1))
    hidden_scr[:, whole:share] = last[:, : share - whole]
    hidden_scr[:, share + whole :] = last[:, share - whole :]
    hidden = hidden_scr[...]
    for i in range(0, out_ref.shape[1], tile):
        cut = slice(i, i + tile)
        second = jnp.concatenate([out_own[:, cut], out_other[:, cut]], axis=0)
        out_ref[:, cut] = jnp.dot(hidden, second, preferred_element_type=jnp.float32)


def expert_rows(rows, in_own, in_other, out_own, out_other):
    count, width = rows.shape
    hidden = in_own.shape[1]
    return pl.pallas_call(
        expert_kernel,
        out_shape=jax.ShapeDtypeStruct((count, width), jnp.float32),
        in_specs=[VMEM] * 5,
        out_specs=VMEM,
        scratch_shapes=[pltpu.VMEM((count, 2 * hidden), jnp.bfloat16)],
        compiler_params=pltpu.CompilerParams(vmem_limit_bytes=32 * 2**20),
        cost_estimate=pl.CostEstimate(
            flops=8 * count * width * hidden,
            bytes_accessed=8 * width * hidden + 6 * count * width,
            transcendentals=2 * count * hidden,
        ),
        name="expert",
    )(rows, in_own, in_other, out_own, out_other)


def along_x(step):
    return "dp", [(x * 2 + c, (x + step) % X * 2 + c) for x in range(X) for c in range(CORES)]


def along_core():
    return "dp", [(i, i ^ 1) for i in range(X * CORES)]


def along_y(step):
    return "expert", [(y * Z + z, (y + step) % Y * Z + z) for y in range(Y) for z in range(Z)]


def flip_z(bit):
    return "expert", [(e, e ^ bit) for e in range(Y * Z)]


def in_order(block, other, place, bit):
    first = (place & bit) == 0
    return jnp.concatenate([jnp.where(first, block, other), jnp.where(first, other, block)])


def in_order_y(got, place):
    order = [got[-k % Y] for k in range(Y)]
    rows = got[0].shape[0]
    start = (Y - place) % Y * rows
    return lax.dynamic_slice_in_dim(jnp.concatenate(order + order), start, Y * rows)


def to_experts(blocks):
    return lax.all_to_all(blocks, "expert", split_axis=0, concat_axis=0, tiled=True)


def on_device(
    tokens, norm_gain, expert_ids, priority, gate_prob, w_in, w_out, text_emb, logit_scale
):
    rows, width = tokens.shape
    half = SLOTS // 2
    dp_place = lax.axis_index("dp")
    places = jnp.stack([dp_place // CORES, dp_place % CORES, lax.axis_index("expert")])

    expert_place = lax.axis_index("expert")
    place_y, place_z = expert_place // Z, expert_place % Z

    text = text_emb.reshape(1, 1, width)
    other = lax.ppermute(text, *flip_z(1))

    outgoing, target = dispatch(
        tokens, norm_gain.reshape(width // LANES, LANES), expert_ids.reshape(1, rows), priority
    )
    outgoing, w_in, w_out = lax.optimization_barrier((outgoing, w_in, w_out))

    weights = (
        w_in[0],
        lax.ppermute(w_in[0], *along_core()),
        w_out[0],
        lax.ppermute(w_out[0], *along_core()),
    )

    own_rows = to_experts(outgoing.reshape(Y * Z, CAP, width)).reshape(SLOTS, width)
    other, own_rows = lax.optimization_barrier((other, own_rows))
    text = in_order(text, other, place_z, 1)

    left_rows = lax.ppermute(own_rows, *along_x(1))
    right_rows = lax.ppermute(own_rows, *along_x(-1))
    own_part = expert_rows(own_rows, *weights)
    other = lax.ppermute(text, *flip_z(2))
    left_rows, right_rows, own_part, other = lax.optimization_barrier(
        (left_rows, right_rows, own_part, other)
    )
    far_rows = jnp.concatenate(
        [
            lax.ppermute(left_rows[:half], *along_x(1)),
            lax.ppermute(right_rows[half:], *along_x(-1)),
        ]
    )
    text = in_order(text, other, place_z, 2)
    other = lax.ppermute(text, *flip_z(4))
    side_part = expert_rows(jnp.concatenate([left_rows, right_rows]), *weights)
    far_rows, side_part, other = lax.optimization_barrier((far_rows, side_part, other))
    far_part = narrow(expert_rows(far_rows, *weights))

    from_right = lax.ppermute(far_part[:half], *along_x(-1))
    from_left = lax.ppermute(far_part[half:], *along_x(1))
    left_sum = jnp.concatenate([side_part[:half] + wide(from_right), side_part[half:SLOTS]])
    right_sum = jnp.concatenate(
        [side_part[SLOTS : SLOTS + half], side_part[SLOTS + half :] + wide(from_left)]
    )
    left_sum, right_sum, other = lax.optimization_barrier(
        (narrow(left_sum), narrow(right_sum), other)
    )
    left_sum = lax.ppermute(left_sum, *along_x(-1))
    right_sum = lax.ppermute(right_sum, *along_x(1))
    text = in_order(text, other, place_z, 4)
    others = [lax.ppermute(text, *along_y(d)) for d in range(1, Y)]
    left_sum, right_sum, *others = lax.optimization_barrier([left_sum, right_sum] + others)
    result = narrow(own_part + wide(left_sum) + wide(right_sum))
    text = in_order_y([text] + others, place_y)

    returned = to_experts(result.reshape(Y * Z, CAP, width)).reshape(SLOTS, width)
    moe_out, pooled = combine(returned, target, gate_prob.reshape(1, rows), tokens)

    text, pooled = lax.optimization_barrier((text.reshape(pooled.shape), pooled))
    texts = [text] + [lax.ppermute(text, *along_x(d)) for d in range(1, X)]
    near = to_experts(pooled.reshape(Y * Z, 1, width)).reshape(pooled.shape)
    texts, near = lax.optimization_barrier((texts, near))
    half = near.shape[0] // 2
    left = lax.ppermute(near, *along_x(1))
    right = lax.ppermute(near, *along_x(-1))
    far = [lax.ppermute(left[:half], *along_x(1)), lax.ppermute(right[half:], *along_x(-1))]
    images = [near, left, right] + far
    loss, grad_image, grad_text = contrast(
        places,
        logit_scale,
        images,
        [lax.ppermute(block, *along_core()) for block in images],
        texts,
        [lax.ppermute(block, *along_core()) for block in texts],
    )
    return (moe_out, loss.reshape(1), grad_image, grad_text)


def solution(mesh):
    in_specs = (
        P(("dp", "expert"), None),
        P(),
        P(("dp", "expert"), None),
        P(("dp", "expert"), None),
        P(("dp", "expert")),
        P("expert", None, "dp"),
        P("expert", "dp", None),
        P(("dp", "expert"), None),
        P(),
    )
    out_specs = (
        P(("dp", "expert"), None),
        P(),
        P(("dp", "expert"), None),
        P(("dp", "expert"), None),
    )
    return jax.shard_map(
        on_device, mesh=mesh, in_specs=in_specs, out_specs=out_specs, check_vma=False
    )
```

```python
import jax
import jax.numpy as jnp
from jax import lax
from jax.experimental import pallas as pl
from jax.experimental.pallas import tpu as pltpu
from jax.sharding import PartitionSpec as P

X, CORES, Y, Z = 4, 2, 4, 8
CAP = 4
LANES, WIDTH = 128, 1280
SLOTS = Y * Z * CAP
PAIRS = X * CORES * Y * Z
VMEM = pl.BlockSpec(memory_space=pltpu.VMEM)
HBM = pl.BlockSpec(memory_space=pltpu.HBM)
SMEM = pl.BlockSpec(memory_space=pltpu.SMEM)


def narrow(values):
    return values.astype(jnp.bfloat16)


def wide(values):
    return values.astype(jnp.float32)


def iota(shape, dim):
    return lax.broadcasted_iota(jnp.int32, shape, dim)


def as_column(row):
    n = row.shape[1]
    same = iota((n, n), 0) == iota((n, n), 1)
    return jnp.sum(jnp.where(same, row, 0.0), axis=1, keepdims=True)


def table_of(target):
    return narrow(wide(iota((SLOTS, target.shape[1]), 0) == target))


def fetch(pairs, sems):
    copies = [
        pltpu.make_async_copy(source, target, sems.at[i]) for i, (source, target) in enumerate(pairs)
    ]
    for copy in copies:
        copy.start()
    for copy in copies:
        copy.wait()


def dispatch_kernel(tokens_hbm, gain_hbm, ids_hbm, ranks_hbm, out_ref, target_ref, *scratch):
    tokens_ref, gain_ref, ids_ref, ranks_ref, sems = scratch
    sources = (tokens_hbm, gain_hbm, ids_hbm, ranks_hbm)
    fetch(list(zip(sources, (tokens_ref, gain_ref, ids_ref, ranks_ref))), sems)
    ids = ids_ref[...]
    base = wide(ids * 256)
    key = base + wide(ranks_ref[...])
    others = as_column(key)
    earlier = (others >= base) & (others < key)
    slots = jnp.sum(wide(earlier), axis=0, keepdims=True).astype(jnp.int32)
    target = jnp.where(slots < CAP, ids * CAP + slots, -1)
    target_ref[...] = target
    values = wide(tokens_ref[...])
    center = values - jnp.mean(values, axis=-1, keepdims=True)
    spread = jnp.mean(center * center, axis=-1, keepdims=True)
    gain = jnp.concatenate([gain_ref[i : i + 1, :] for i in range(gain_ref.shape[0])], axis=1)
    normed = narrow(center * lax.rsqrt(spread + 1e-06) * gain)
    out_ref[...] = narrow(
        jnp.dot(table_of(target), normed, preferred_element_type=jnp.float32)
    )


def dispatch(tokens, gain, ids, ranks):
    rows, width = tokens.shape
    inputs = (tokens, gain, ids, ranks)
    return pl.pallas_call(
        dispatch_kernel,
        out_shape=(
            jax.ShapeDtypeStruct((SLOTS, width), jnp.bfloat16),
            jax.ShapeDtypeStruct((1, rows), jnp.int32),
        ),
        in_specs=[HBM] * 4,
        out_specs=(VMEM, VMEM),
        scratch_shapes=[pltpu.VMEM(x.shape, x.dtype) for x in inputs]
        + [pltpu.SemaphoreType.DMA((len(inputs),))],
        compiler_params=pltpu.CompilerParams(vmem_limit_bytes=64 * 2**20),
        name="dispatch",
    )(*inputs)


def combine_kernel(returned_ref, target_ref, gate_ref, tokens_ref, out_ref, pooled_ref):
    expert_part = lax.dot_general(
        table_of(target_ref[...]),
        returned_ref[...],
        (((0,), (0,)), ((), ())),
        preferred_element_type=jnp.float32,
    )
    moe_out = narrow(wide(tokens_ref[...]) + as_column(gate_ref[...]) * expert_part)
    out_ref[...] = moe_out
    pooled = jnp.mean(wide(moe_out), axis=0, keepdims=True)
    pieces = pooled.shape[1] // LANES
    for index in range(pieces):
        piece = pooled[:, index * LANES : (index + 1) * LANES]
        pooled_ref[pl.ds(index, Y * Z, stride=pieces), :] = jnp.broadcast_to(piece, (Y * Z, LANES))


def combine(returned, target, gate, tokens):
    rows, width = tokens.shape
    return pl.pallas_call(
        combine_kernel,
        out_shape=(
            jax.ShapeDtypeStruct((rows, width), jnp.bfloat16),
            jax.ShapeDtypeStruct((Y * Z * width // LANES, LANES), jnp.float32),
        ),
        in_specs=[VMEM] * 4,
        out_specs=(VMEM, VMEM),
        name="combine",
    )(returned, target, gate, tokens)


def full_rows(ref, first=0, every=1):
    pieces = WIDTH // LANES
    step = pieces * every
    count = ref.shape[0] // step
    return jnp.concatenate(
        [ref[pl.ds(first * pieces + i, count, stride=step), :] for i in range(pieces)], axis=1
    )


def contrast_kernel(place_ref, scale_ref, text_ref, *refs):
    images, texts = (refs[:5], refs[5:10]), (refs[10:14], refs[14:18])
    loss_ref, image_ref, dtext_ref, image_scr, text_scr = refs[18:]
    place_x, core, expert = place_ref[0], place_ref[1], place_ref[2]
    me = (place_x * CORES + core) * (Y * Z) + expert
    scale = scale_ref[0]

    def put(scratch, step, c, first, rows):
        square = jnp.sum(rows * rows, axis=-1, keepdims=True)
        x = (place_x + step) & (X - 1)
        start = pl.multiple_of((x * CORES + c) * (Y * Z) + first, 8)
        scratch[pl.ds(start, rows.shape[0]), :] = rows / jnp.sqrt(square + 1e-06)

    half = Y * Z // 2
    for side in range(CORES):
        c = core + side - 2 * core * side
        for ref, step, first in zip(images[side], (0, 3, 1, 2, 2), (0, 0, 0, 0, half)):
            put(image_scr, step, c, first, full_rows(ref))
    for own_ref, other_ref, step in zip(*texts, (0, 3, 2, 1)):
        for c in range(CORES):
            own_rows, other_rows = full_rows(own_ref, c, CORES), full_rows(other_ref, c, CORES)
            put(text_scr, step, c, 0, jnp.where(core == 1, own_rows, other_rows))
    image_unit = image_scr[...]
    text_unit = text_scr[...]
    logits = scale * lax.dot_general(
        image_unit,
        text_unit,
        (((1,), (1,)), ((), ())),
        precision=lax.Precision.HIGHEST,
        preferred_element_type=jnp.float32,
    )
    row_max = jnp.max(logits, axis=1, keepdims=True)
    col_max = jnp.max(logits, axis=0, keepdims=True)
    row_lse = row_max + jnp.log(jnp.sum(jnp.exp(logits - row_max), axis=1, keepdims=True))
    col_lse = col_max + jnp.log(jnp.sum(jnp.exp(logits - col_max), axis=0, keepdims=True))
    rows_at, cols_at = iota(logits.shape, 0), iota(logits.shape, 1)
    same = rows_at == cols_at
    trace = jnp.sum(jnp.where(same, logits, 0.0), axis=(0, 1), keepdims=True)
    total = jnp.sum(row_lse, axis=0, keepdims=True) + jnp.sum(col_lse, axis=1, keepdims=True)
    loss_ref[...] = (total - 2.0 * trace) / (2.0 * PAIRS)
    grad = jnp.exp(logits - row_lse) + jnp.exp(logits - col_lse) - 2.0 * wide(same)
    grad = grad / (2.0 * PAIRS)
    own_col = jnp.sum(jnp.where(cols_at == me, grad, 0.0), axis=1, keepdims=True)
    own_row = as_column(jnp.sum(jnp.where(rows_at == me, grad, 0.0), axis=0, keepdims=True))
    d_image = scale * jnp.sum(own_row * text_unit, axis=0, keepdims=True)
    d_text = scale * jnp.sum(own_col * image_unit, axis=0, keepdims=True)

    def back(unit, radius, upstream):
        along = jnp.sum(unit * upstream, axis=-1, keepdims=True)
        return (upstream - unit * along) / radius

    def own(rows):
        radius = jnp.sqrt(jnp.sum(rows * rows, axis=-1, keepdims=True) + 1e-06)
        return rows / radius, radius

    def own_row(ref):
        pieces = WIDTH // LANES
        return jnp.concatenate(
            [ref[pl.ds(expert * pieces + i, 1), :] for i in range(pieces)], axis=1
        )

    image_ref[...] = back(*own(own_row(images[0][0])), d_image)
    dtext_ref[...] = back(*own(text_ref[...]), d_text)


def contrast(places, scale, text, images, other_images, texts, other_texts):
    row = jax.ShapeDtypeStruct((1, WIDTH), jnp.float32)
    return pl.pallas_call(
        contrast_kernel,
        out_shape=(jax.ShapeDtypeStruct((1, 1), jnp.float32), row, row),
        in_specs=[SMEM, SMEM] + [VMEM] * 19,
        out_specs=(VMEM, VMEM, VMEM),
        scratch_shapes=[pltpu.VMEM((PAIRS, WIDTH), jnp.float32)] * 2,
        compiler_params=pltpu.CompilerParams(vmem_limit_bytes=32 * 2**20),
        name="contrast",
    )(places, scale, text, *images, *other_images, *texts, *other_texts)


def expert_kernel(rows_ref, in_own, in_other, out_own, out_other, out_ref, hidden_scr):
    rows = rows_ref[...]
    share = in_own.shape[1]
    tile = 2 * LANES
    whole = share // tile * tile
    cuts = [slice(i, i + tile) for i in range(0, whole, tile)]

    def hidden_of(first):
        hidden = jax.nn.gelu(jnp.dot(rows, first, preferred_element_type=jnp.float32))
        return narrow(hidden)

    for cut in cuts:
        hidden_scr[:, cut] = hidden_of(in_own[:, cut])
        hidden_scr[:, share + cut.start : share + cut.stop] = hidden_of(in_other[:, cut])
    last = hidden_of(jnp.concatenate([in_own[:, whole:], in_other[:, whole:]], axis=1))
    hidden_scr[:, whole:share] = last[:, : share - whole]
    hidden_scr[:, share + whole :] = last[:, share - whole :]
    hidden = hidden_scr[...]
    for i in range(0, out_ref.shape[1], tile):
        cut = slice(i, i + tile)
        second = jnp.concatenate([out_own[:, cut], out_other[:, cut]], axis=0)
        out_ref[:, cut] = jnp.dot(hidden, second, preferred_element_type=jnp.float32)


def expert_rows(rows, in_own, in_other, out_own, out_other):
    count, width = rows.shape
    hidden = in_own.shape[1]
    return pl.pallas_call(
        expert_kernel,
        out_shape=jax.ShapeDtypeStruct((count, width), jnp.float32),
        in_specs=[VMEM] * 5,
        out_specs=VMEM,
        scratch_shapes=[pltpu.VMEM((count, 2 * hidden), jnp.bfloat16)],
        compiler_params=pltpu.CompilerParams(vmem_limit_bytes=32 * 2**20),
        cost_estimate=pl.CostEstimate(
            flops=8 * count * width * hidden,
            bytes_accessed=8 * width * hidden + 6 * count * width,
            transcendentals=2 * count * hidden,
        ),
        name="expert",
    )(rows, in_own, in_other, out_own, out_other)


def along_x(step):
    return "dp", [(x * 2 + c, (x + step) % X * 2 + c) for x in range(X) for c in range(CORES)]


def along_core():
    return "dp", [(i, i ^ 1) for i in range(X * CORES)]


def text_pairs(move):
    pairs = []
    for x in range(X):
        for y in range(Y):
            for z in range(Z):
                to_x, to_y, to_z = move(x, y, z)
                source = (x * CORES + 1) * Y * Z + y * Z + z
                pairs.append((source, (to_x * CORES + 1) * Y * Z + to_y * Z + to_z))
    return ("dp", "expert"), pairs


def text_z(bit):
    return text_pairs(lambda x, y, z: (x, y, z ^ bit))


def text_y(step):
    return text_pairs(lambda x, y, z: (x, (y + step) % Y, z))


def text_x(step):
    return text_pairs(lambda x, y, z: ((x + step) % X, y, z))


def to_core(core):
    return "dp", [(x * CORES + 1 - core, x * CORES + core) for x in range(X)]


def in_order(block, other, place, bit):
    first = (place & bit) == 0
    return jnp.concatenate([jnp.where(first, block, other), jnp.where(first, other, block)])


def in_order_y(got, place):
    order = [got[-k % Y] for k in range(Y)]
    rows = got[0].shape[0]
    start = (Y - place) % Y * rows
    return lax.dynamic_slice_in_dim(jnp.concatenate(order + order), start, Y * rows)


def to_experts(blocks):
    return lax.all_to_all(blocks, "expert", split_axis=0, concat_axis=0, tiled=True)


def on_device(
    tokens, norm_gain, expert_ids, priority, gate_prob, w_in, w_out, text_emb, logit_scale
):
    rows, width = tokens.shape
    half = SLOTS // 2
    dp_place = lax.axis_index("dp")
    places = jnp.stack([dp_place // CORES, dp_place % CORES, lax.axis_index("expert")])

    expert_place = lax.axis_index("expert")
    place_y, place_z = expert_place // Z, expert_place % Z

    text = text_emb.reshape(1, 1, width)
    text = jnp.concatenate([lax.ppermute(text, *to_core(1)), text])

    outgoing, target = dispatch(
        tokens, norm_gain.reshape(width // LANES, LANES), expert_ids.reshape(1, rows), priority
    )
    text, outgoing, w_in, w_out = lax.optimization_barrier((text, outgoing, w_in, w_out))

    weights = (
        w_in[0],
        lax.ppermute(w_in[0], *along_core()),
        w_out[0],
        lax.ppermute(w_out[0], *along_core()),
    )

    own_rows = to_experts(outgoing.reshape(Y * Z, CAP, width)).reshape(SLOTS, width)
    text, own_rows = lax.optimization_barrier((text, own_rows))

    left_rows = lax.ppermute(own_rows, *along_x(1))
    right_rows = lax.ppermute(own_rows, *along_x(-1))
    own_part = expert_rows(own_rows, *weights)
    other = lax.ppermute(text, *text_z(1))
    left_rows, right_rows, own_part, other = lax.optimization_barrier(
        (left_rows, right_rows, own_part, other)
    )
    far_rows = jnp.concatenate(
        [
            lax.ppermute(left_rows[:half], *along_x(1)),
            lax.ppermute(right_rows[half:], *along_x(-1)),
        ]
    )
    text = in_order(text, other, place_z, 1)
    other = lax.ppermute(text, *text_z(2))
    side_part = expert_rows(jnp.concatenate([left_rows, right_rows]), *weights)
    far_rows, side_part, other = lax.optimization_barrier((far_rows, side_part, other))
    far_part = narrow(expert_rows(far_rows, *weights))

    from_right = lax.ppermute(far_part[:half], *along_x(-1))
    from_left = lax.ppermute(far_part[half:], *along_x(1))
    text = in_order(text, other, place_z, 2)
    other = lax.ppermute(text, *text_z(4))
    from_left, from_right, other = lax.optimization_barrier((from_left, from_right, other))
    left_sum = jnp.concatenate([side_part[:half] + wide(from_right), side_part[half:SLOTS]])
    right_sum = jnp.concatenate(
        [side_part[SLOTS : SLOTS + half], side_part[SLOTS + half :] + wide(from_left)]
    )
    left_sum, right_sum, other = lax.optimization_barrier(
        (narrow(left_sum), narrow(right_sum), other)
    )
    left_sum = lax.ppermute(left_sum, *along_x(-1))
    right_sum = lax.ppermute(right_sum, *along_x(1))
    text = in_order(text, other, place_z, 4)
    others = [lax.ppermute(text, *text_y(d)) for d in range(1, Y)]
    left_sum, right_sum, *others = lax.optimization_barrier([left_sum, right_sum] + others)
    result = narrow(own_part + wide(left_sum) + wide(right_sum))
    text = in_order_y([text] + others, place_y)

    returned = to_experts(result.reshape(Y * Z, CAP, width)).reshape(SLOTS, width)
    moe_out, pooled = combine(returned, target, gate_prob.reshape(1, rows), tokens)

    text, pooled = lax.optimization_barrier((text.reshape(-1, LANES), pooled))
    texts = [text] + [lax.ppermute(text, *text_x(d)) for d in range(1, X)]
    near = to_experts(pooled.reshape(Y * Z, 1, width)).reshape(pooled.shape)
    texts, near = lax.optimization_barrier((texts, near))
    half = near.shape[0] // 2
    left = lax.ppermute(near, *along_x(1))
    right = lax.ppermute(near, *along_x(-1))
    far = [lax.ppermute(left[:half], *along_x(1)), lax.ppermute(right[half:], *along_x(-1))]
    images = [near, left, right] + far
    loss, grad_image, grad_text = contrast(
        places,
        logit_scale,
        text_emb,
        images,
        [lax.ppermute(block, *along_core()) for block in images],
        texts,
        [lax.ppermute(block, *to_core(0)) for block in texts],
    )
    return (moe_out, loss.reshape(1), grad_image, grad_text)


def solution(mesh):
    in_specs = (
        P(("dp", "expert"), None),
        P(),
        P(("dp", "expert"), None),
        P(("dp", "expert"), None),
        P(("dp", "expert")),
        P("expert", None, "dp"),
        P("expert", "dp", None),
        P(("dp", "expert"), None),
        P(),
    )
    out_specs = (
        P(("dp", "expert"), None),
        P(),
        P(("dp", "expert"), None),
        P(("dp", "expert"), None),
    )
    return jax.shard_map(
        on_device, mesh=mesh, in_specs=in_specs, out_specs=out_specs, check_vma=False
    )
```

```python
import jax
import jax.numpy as jnp
from jax import lax
from jax.experimental import pallas as pl
from jax.experimental.pallas import tpu as pltpu
from jax.sharding import PartitionSpec as P

X, CORES, Y, Z = 4, 2, 4, 8
CAP = 4
LANES, WIDTH = 128, 1280
SLOTS = Y * Z * CAP
PAIRS = X * CORES * Y * Z
VMEM = pl.BlockSpec(memory_space=pltpu.VMEM)
HBM = pl.BlockSpec(memory_space=pltpu.HBM)
SMEM = pl.BlockSpec(memory_space=pltpu.SMEM)


def narrow(values):
    return values.astype(jnp.bfloat16)


def wide(values):
    return values.astype(jnp.float32)


def iota(shape, dim):
    return lax.broadcasted_iota(jnp.int32, shape, dim)


def as_column(row):
    n = row.shape[1]
    same = iota((n, n), 0) == iota((n, n), 1)
    return jnp.sum(jnp.where(same, row, 0.0), axis=1, keepdims=True)


def table_of(target):
    return narrow(wide(iota((SLOTS, target.shape[1]), 0) == target))


def fetch(pairs, sems):
    copies = [
        pltpu.make_async_copy(source, target, sems.at[i]) for i, (source, target) in enumerate(pairs)
    ]
    for copy in copies:
        copy.start()
    for copy in copies:
        copy.wait()


def dispatch_kernel(tokens_hbm, gain_hbm, ids_hbm, ranks_hbm, out_ref, target_ref, *scratch):
    tokens_ref, gain_ref, ids_ref, ranks_ref, sems = scratch
    sources = (tokens_hbm, gain_hbm, ids_hbm, ranks_hbm)
    fetch(list(zip(sources, (tokens_ref, gain_ref, ids_ref, ranks_ref))), sems)
    ids = ids_ref[...]
    base = wide(ids * 256)
    key = base + wide(ranks_ref[...])
    others = as_column(key)
    earlier = (others >= base) & (others < key)
    slots = jnp.sum(wide(earlier), axis=0, keepdims=True).astype(jnp.int32)
    target = jnp.where(slots < CAP, ids * CAP + slots, -1)
    target_ref[...] = target
    values = wide(tokens_ref[...])
    center = values - jnp.mean(values, axis=-1, keepdims=True)
    spread = jnp.mean(center * center, axis=-1, keepdims=True)
    gain = jnp.concatenate([gain_ref[i : i + 1, :] for i in range(gain_ref.shape[0])], axis=1)
    normed = narrow(center * lax.rsqrt(spread + 1e-06) * gain)
    out_ref[...] = narrow(
        jnp.dot(table_of(target), normed, preferred_element_type=jnp.float32)
    )


def dispatch(tokens, gain, ids, ranks):
    rows, width = tokens.shape
    inputs = (tokens, gain, ids, ranks)
    return pl.pallas_call(
        dispatch_kernel,
        out_shape=(
            jax.ShapeDtypeStruct((SLOTS, width), jnp.bfloat16),
            jax.ShapeDtypeStruct((1, rows), jnp.int32),
        ),
        in_specs=[HBM] * 4,
        out_specs=(VMEM, VMEM),
        scratch_shapes=[pltpu.VMEM(x.shape, x.dtype) for x in inputs]
        + [pltpu.SemaphoreType.DMA((len(inputs),))],
        compiler_params=pltpu.CompilerParams(vmem_limit_bytes=64 * 2**20),
        name="dispatch",
    )(*inputs)


def combine_kernel(
    returned_ref, target_ref, gate_ref, tokens_ref, text_ref, out_ref, pair_ref
):
    expert_part = lax.dot_general(
        table_of(target_ref[...]),
        returned_ref[...],
        (((0,), (0,)), ((), ())),
        preferred_element_type=jnp.float32,
    )
    moe_out = narrow(wide(tokens_ref[...]) + as_column(gate_ref[...]) * expert_part)
    out_ref[...] = moe_out
    pooled = jnp.mean(wide(moe_out), axis=0, keepdims=True)
    pair = jnp.concatenate([pooled, text_ref[...]], axis=1)
    pieces = pair.shape[1] // LANES
    for index in range(pieces):
        piece = pair[:, index * LANES : (index + 1) * LANES]
        pair_ref[pl.ds(index, Y * Z, stride=pieces), :] = jnp.broadcast_to(piece, (Y * Z, LANES))


def combine(returned, target, gate, tokens, text):
    rows, width = tokens.shape
    return pl.pallas_call(
        combine_kernel,
        out_shape=(
            jax.ShapeDtypeStruct((rows, width), jnp.bfloat16),
            jax.ShapeDtypeStruct((Y * Z * 2 * width // LANES, LANES), jnp.float32),
        ),
        in_specs=[VMEM] * 5,
        out_specs=(VMEM, VMEM),
        name="combine",
    )(returned, target, gate, tokens, text)


def full_rows(ref, which):
    pieces = WIDTH // LANES
    count = ref.shape[0] // (2 * pieces)
    return jnp.concatenate(
        [ref[pl.ds(which * pieces + i, count, stride=2 * pieces), :] for i in range(pieces)],
        axis=1,
    )


def contrast_kernel(place_ref, scale_ref, *refs):
    blocks = (refs[:5], refs[5:10])
    loss_ref, image_ref, dtext_ref, image_scr, text_scr = refs[10:]
    place_x, core, expert = place_ref[0], place_ref[1], place_ref[2]
    me = (place_x * CORES + core) * (Y * Z) + expert
    scale = scale_ref[0]

    half = Y * Z // 2
    for side in range(CORES):
        c = core + side - 2 * core * side
        for ref, step, first in zip(blocks[side], (0, 3, 1, 2, 2), (0, 0, 0, 0, half)):
            x = (place_x + step) & (X - 1)
            start = pl.multiple_of((x * CORES + c) * (Y * Z) + first, 8)
            for which, scratch in enumerate((image_scr, text_scr)):
                rows = full_rows(ref, which)
                square = jnp.sum(rows * rows, axis=-1, keepdims=True)
                scratch[pl.ds(start, rows.shape[0]), :] = rows / jnp.sqrt(square + 1e-06)
    image_unit = image_scr[...]
    text_unit = text_scr[...]
    logits = scale * lax.dot_general(
        image_unit,
        text_unit,
        (((1,), (1,)), ((), ())),
        precision=lax.Precision.HIGHEST,
        preferred_element_type=jnp.float32,
    )
    row_max = jnp.max(logits, axis=1, keepdims=True)
    col_max = jnp.max(logits, axis=0, keepdims=True)
    row_lse = row_max + jnp.log(jnp.sum(jnp.exp(logits - row_max), axis=1, keepdims=True))
    col_lse = col_max + jnp.log(jnp.sum(jnp.exp(logits - col_max), axis=0, keepdims=True))
    rows_at, cols_at = iota(logits.shape, 0), iota(logits.shape, 1)
    same = rows_at == cols_at
    trace = jnp.sum(jnp.where(same, logits, 0.0), axis=(0, 1), keepdims=True)
    total = jnp.sum(row_lse, axis=0, keepdims=True) + jnp.sum(col_lse, axis=1, keepdims=True)
    loss_ref[...] = (total - 2.0 * trace) / (2.0 * PAIRS)
    grad = jnp.exp(logits - row_lse) + jnp.exp(logits - col_lse) - 2.0 * wide(same)
    grad = grad / (2.0 * PAIRS)
    own_col = jnp.sum(jnp.where(cols_at == me, grad, 0.0), axis=1, keepdims=True)
    own_row = as_column(jnp.sum(jnp.where(rows_at == me, grad, 0.0), axis=0, keepdims=True))
    d_image = scale * jnp.sum(own_row * text_unit, axis=0, keepdims=True)
    d_text = scale * jnp.sum(own_col * image_unit, axis=0, keepdims=True)

    def back(unit, radius, upstream):
        along = jnp.sum(unit * upstream, axis=-1, keepdims=True)
        return (upstream - unit * along) / radius

    def own(rows):
        radius = jnp.sqrt(jnp.sum(rows * rows, axis=-1, keepdims=True) + 1e-06)
        return rows / radius, radius

    def own_row(which):
        pieces = WIDTH // LANES
        first = (2 * expert + which) * pieces
        return jnp.concatenate(
            [blocks[0][0][pl.ds(first + i, 1), :] for i in range(pieces)], axis=1
        )

    image_ref[...] = back(*own(own_row(0)), d_image)
    dtext_ref[...] = back(*own(own_row(1)), d_text)


def contrast(places, scale, blocks, other_blocks):
    row = jax.ShapeDtypeStruct((1, WIDTH), jnp.float32)
    return pl.pallas_call(
        contrast_kernel,
        out_shape=(jax.ShapeDtypeStruct((1, 1), jnp.float32), row, row),
        in_specs=[SMEM, SMEM] + [VMEM] * 10,
        out_specs=(VMEM, VMEM, VMEM),
        scratch_shapes=[pltpu.VMEM((PAIRS, WIDTH), jnp.float32)] * 2,
        compiler_params=pltpu.CompilerParams(vmem_limit_bytes=32 * 2**20),
        name="contrast",
    )(places, scale, *blocks, *other_blocks)


def expert_kernel(rows_ref, in_own, in_other, out_own, out_other, out_ref, hidden_scr):
    rows = rows_ref[...]
    share = in_own.shape[1]
    tile = 2 * LANES
    whole = share // tile * tile
    cuts = [slice(i, i + tile) for i in range(0, whole, tile)]

    def hidden_of(first):
        hidden = jax.nn.gelu(jnp.dot(rows, first, preferred_element_type=jnp.float32))
        return narrow(hidden)

    for cut in cuts:
        hidden_scr[:, cut] = hidden_of(in_own[:, cut])
        hidden_scr[:, share + cut.start : share + cut.stop] = hidden_of(in_other[:, cut])
    last = hidden_of(jnp.concatenate([in_own[:, whole:], in_other[:, whole:]], axis=1))
    hidden_scr[:, whole:share] = last[:, : share - whole]
    hidden_scr[:, share + whole :] = last[:, share - whole :]
    hidden = hidden_scr[...]
    for i in range(0, out_ref.shape[1], tile):
        cut = slice(i, i + tile)
        second = jnp.concatenate([out_own[:, cut], out_other[:, cut]], axis=0)
        out_ref[:, cut] = jnp.dot(hidden, second, preferred_element_type=jnp.float32)


def expert_rows(rows, in_own, in_other, out_own, out_other):
    count, width = rows.shape
    hidden = in_own.shape[1]
    return pl.pallas_call(
        expert_kernel,
        out_shape=jax.ShapeDtypeStruct((count, width), jnp.float32),
        in_specs=[VMEM] * 5,
        out_specs=VMEM,
        scratch_shapes=[pltpu.VMEM((count, 2 * hidden), jnp.bfloat16)],
        compiler_params=pltpu.CompilerParams(vmem_limit_bytes=32 * 2**20),
        cost_estimate=pl.CostEstimate(
            flops=8 * count * width * hidden,
            bytes_accessed=8 * width * hidden + 6 * count * width,
            transcendentals=2 * count * hidden,
        ),
        name="expert",
    )(rows, in_own, in_other, out_own, out_other)


def along_x(step):
    return "dp", [(x * 2 + c, (x + step) % X * 2 + c) for x in range(X) for c in range(CORES)]


def along_core():
    return "dp", [(i, i ^ 1) for i in range(X * CORES)]


def to_experts(blocks):
    return lax.all_to_all(blocks, "expert", split_axis=0, concat_axis=0, tiled=True)


def on_device(
    tokens, norm_gain, expert_ids, priority, gate_prob, w_in, w_out, text_emb, logit_scale
):
    rows, width = tokens.shape
    half = SLOTS // 2
    dp_place = lax.axis_index("dp")
    places = jnp.stack([dp_place // CORES, dp_place % CORES, lax.axis_index("expert")])

    outgoing, target = dispatch(
        tokens, norm_gain.reshape(width // LANES, LANES), expert_ids.reshape(1, rows), priority
    )
    outgoing, w_in, w_out = lax.optimization_barrier((outgoing, w_in, w_out))

    weights = (
        w_in[0],
        lax.ppermute(w_in[0], *along_core()),
        w_out[0],
        lax.ppermute(w_out[0], *along_core()),
    )

    own_rows = to_experts(outgoing.reshape(Y * Z, CAP, width)).reshape(SLOTS, width)

    left_rows = lax.ppermute(own_rows, *along_x(1))
    right_rows = lax.ppermute(own_rows, *along_x(-1))
    own_part = expert_rows(own_rows, *weights)
    left_rows, right_rows, own_part = lax.optimization_barrier((left_rows, right_rows, own_part))
    far_rows = jnp.concatenate(
        [
            lax.ppermute(left_rows[:half], *along_x(1)),
            lax.ppermute(right_rows[half:], *along_x(-1)),
        ]
    )
    side_part = expert_rows(jnp.concatenate([left_rows, right_rows]), *weights)
    far_rows, side_part = lax.optimization_barrier((far_rows, side_part))
    far_part = narrow(expert_rows(far_rows, *weights))

    from_right = lax.ppermute(far_part[:half], *along_x(-1))
    from_left = lax.ppermute(far_part[half:], *along_x(1))
    left_sum = jnp.concatenate([side_part[:half] + wide(from_right), side_part[half:SLOTS]])
    right_sum = jnp.concatenate(
        [side_part[SLOTS : SLOTS + half], side_part[SLOTS + half :] + wide(from_left)]
    )
    left_sum = lax.ppermute(narrow(left_sum), *along_x(-1))
    right_sum = lax.ppermute(narrow(right_sum), *along_x(1))
    result = narrow(own_part + wide(left_sum) + wide(right_sum))

    returned = to_experts(result.reshape(Y * Z, CAP, width)).reshape(SLOTS, width)
    moe_out, pair = combine(returned, target, gate_prob.reshape(1, rows), tokens, text_emb)

    near = to_experts(pair.reshape(Y * Z, 1, 2 * width)).reshape(pair.shape)
    half = near.shape[0] // 2
    left = lax.ppermute(near, *along_x(1))
    right = lax.ppermute(near, *along_x(-1))
    far = [lax.ppermute(left[:half], *along_x(1)), lax.ppermute(right[half:], *along_x(-1))]
    blocks = [near, left, right] + far
    loss, grad_image, grad_text = contrast(
        places,
        logit_scale,
        blocks,
        [lax.ppermute(block, *along_core()) for block in blocks],
    )
    return (moe_out, loss.reshape(1), grad_image, grad_text)


def solution(mesh):
    in_specs = (
        P(("dp", "expert"), None),
        P(),
        P(("dp", "expert"), None),
        P(("dp", "expert"), None),
        P(("dp", "expert")),
        P("expert", None, "dp"),
        P("expert", "dp", None),
        P(("dp", "expert"), None),
        P(),
    )
    out_specs = (
        P(("dp", "expert"), None),
        P(),
        P(("dp", "expert"), None),
        P(("dp", "expert"), None),
    )
    return jax.shard_map(
        on_device, mesh=mesh, in_specs=in_specs, out_specs=out_specs, check_vma=False
    )
```

```python
import jax
import jax.numpy as jnp
from jax import lax
from jax.experimental import pallas as pl
from jax.experimental.pallas import tpu as pltpu
from jax.sharding import PartitionSpec as P

X, CORES, Y, Z = 4, 2, 4, 8
CAP = 4
LANES, WIDTH = 128, 1280
SLOTS = Y * Z * CAP
PAIRS = X * CORES * Y * Z
VMEM = pl.BlockSpec(memory_space=pltpu.VMEM)
SMEM = pl.BlockSpec(memory_space=pltpu.SMEM)


def narrow(values):
    return values.astype(jnp.bfloat16)


def wide(values):
    return values.astype(jnp.float32)


def iota(shape, dim):
    return lax.broadcasted_iota(jnp.int32, shape, dim)


def as_column(row):
    n = row.shape[1]
    same = iota((n, n), 0) == iota((n, n), 1)
    return jnp.sum(jnp.where(same, row, 0.0), axis=1, keepdims=True)


def table_of(target):
    return narrow(wide(iota((SLOTS, target.shape[1]), 0) == target))


def dispatch_kernel(tokens_ref, gain_ref, key_ref, out_ref, target_ref):
    whole_key = key_ref[...]
    ids = whole_key >> 8
    base, key = wide(ids * 256), wide(whole_key)
    others = as_column(key)
    earlier = (others >= base) & (others < key)
    slots = jnp.sum(wide(earlier), axis=0, keepdims=True).astype(jnp.int32)
    target = jnp.where(slots < CAP, ids * CAP + slots, -1)
    target_ref[...] = target
    values = wide(tokens_ref[...])
    center = values - jnp.mean(values, axis=-1, keepdims=True)
    spread = jnp.mean(center * center, axis=-1, keepdims=True)
    gain = jnp.concatenate([gain_ref[i : i + 1, :] for i in range(gain_ref.shape[0])], axis=1)
    normed = narrow(center * lax.rsqrt(spread + 1e-06) * gain)
    out_ref[...] = narrow(
        jnp.dot(table_of(target), normed, preferred_element_type=jnp.float32)
    )


def dispatch(tokens, gain, key):
    rows, width = tokens.shape
    return pl.pallas_call(
        dispatch_kernel,
        out_shape=(
            jax.ShapeDtypeStruct((SLOTS, width), jnp.bfloat16),
            jax.ShapeDtypeStruct((1, rows), jnp.int32),
        ),
        in_specs=[VMEM] * 3,
        out_specs=(VMEM, VMEM),
        compiler_params=pltpu.CompilerParams(vmem_limit_bytes=24 * 2**20),
        name="dispatch",
    )(tokens, gain, key)


def combine_kernel(
    returned_ref, target_ref, gate_ref, tokens_ref, text_ref, out_ref, pair_ref
):
    expert_part = lax.dot_general(
        table_of(target_ref[...]),
        returned_ref[...],
        (((0,), (0,)), ((), ())),
        preferred_element_type=jnp.float32,
    )
    moe_out = narrow(wide(tokens_ref[...]) + as_column(gate_ref[...]) * expert_part)
    out_ref[...] = moe_out
    pooled = jnp.mean(wide(moe_out), axis=0, keepdims=True)
    pair = jnp.concatenate([pooled, text_ref[...]], axis=1)
    pieces = pair.shape[1] // LANES
    for index in range(pieces):
        piece = pair[:, index * LANES : (index + 1) * LANES]
        pair_ref[pl.ds(index, Y * Z, stride=pieces), :] = jnp.broadcast_to(piece, (Y * Z, LANES))


def combine(returned, target, gate, tokens, text):
    rows, width = tokens.shape
    return pl.pallas_call(
        combine_kernel,
        out_shape=(
            jax.ShapeDtypeStruct((rows, width), jnp.bfloat16),
            jax.ShapeDtypeStruct((Y * Z * 2 * width // LANES, LANES), jnp.float32),
        ),
        in_specs=[VMEM] * 5,
        out_specs=(VMEM, VMEM),
        compiler_params=pltpu.CompilerParams(vmem_limit_bytes=24 * 2**20),
        name="combine",
    )(returned, target, gate, tokens, text)


def full_rows(ref, which):
    pieces = WIDTH // LANES
    count = ref.shape[0] // (2 * pieces)
    return jnp.concatenate(
        [ref[pl.ds(which * pieces + i, count, stride=2 * pieces), :] for i in range(pieces)],
        axis=1,
    )


def contrast_kernel(place_ref, scale_ref, *refs):
    blocks = (refs[:5], refs[5:10])
    loss_ref, image_ref, dtext_ref, image_scr, text_scr = refs[10:]
    place_x, core, expert = place_ref[0], place_ref[1], place_ref[2]
    me = (place_x * CORES + core) * (Y * Z) + expert
    scale = scale_ref[0]

    half = Y * Z // 2
    for side in range(CORES):
        c = core + side - 2 * core * side
        for ref, step, first in zip(blocks[side], (0, 3, 1, 2, 2), (0, 0, 0, 0, half)):
            x = (place_x + step) & (X - 1)
            start = pl.multiple_of((x * CORES + c) * (Y * Z) + first, 8)
            for which, scratch in enumerate((image_scr, text_scr)):
                rows = full_rows(ref, which)
                square = jnp.sum(rows * rows, axis=-1, keepdims=True)
                scratch[pl.ds(start, rows.shape[0]), :] = rows / jnp.sqrt(square + 1e-06)
    image_unit = image_scr[...]
    text_unit = text_scr[...]
    logits = scale * lax.dot_general(
        image_unit,
        text_unit,
        (((1,), (1,)), ((), ())),
        precision=lax.Precision.HIGHEST,
        preferred_element_type=jnp.float32,
    )
    row_max = jnp.max(logits, axis=1, keepdims=True)
    col_max = jnp.max(logits, axis=0, keepdims=True)
    row_lse = row_max + jnp.log(jnp.sum(jnp.exp(logits - row_max), axis=1, keepdims=True))
    col_lse = col_max + jnp.log(jnp.sum(jnp.exp(logits - col_max), axis=0, keepdims=True))
    rows_at, cols_at = iota(logits.shape, 0), iota(logits.shape, 1)
    same = rows_at == cols_at
    trace = jnp.sum(jnp.where(same, logits, 0.0), axis=(0, 1), keepdims=True)
    total = jnp.sum(row_lse, axis=0, keepdims=True) + jnp.sum(col_lse, axis=1, keepdims=True)
    loss_ref[...] = (total - 2.0 * trace) / (2.0 * PAIRS)
    grad = jnp.exp(logits - row_lse) + jnp.exp(logits - col_lse) - 2.0 * wide(same)
    grad = grad / (2.0 * PAIRS)
    own_col = jnp.sum(jnp.where(cols_at == me, grad, 0.0), axis=1, keepdims=True)
    own_row = as_column(jnp.sum(jnp.where(rows_at == me, grad, 0.0), axis=0, keepdims=True))
    d_image = scale * jnp.sum(own_row * text_unit, axis=0, keepdims=True)
    d_text = scale * jnp.sum(own_col * image_unit, axis=0, keepdims=True)

    def back(unit, radius, upstream):
        along = jnp.sum(unit * upstream, axis=-1, keepdims=True)
        return (upstream - unit * along) / radius

    def own(rows):
        radius = jnp.sqrt(jnp.sum(rows * rows, axis=-1, keepdims=True) + 1e-06)
        return rows / radius, radius

    def own_row(which):
        pieces = WIDTH // LANES
        first = (2 * expert + which) * pieces
        return jnp.concatenate(
            [blocks[0][0][pl.ds(first + i, 1), :] for i in range(pieces)], axis=1
        )

    image_ref[...] = back(*own(own_row(0)), d_image)
    dtext_ref[...] = back(*own(own_row(1)), d_text)


def contrast(places, scale, blocks, other_blocks):
    row = jax.ShapeDtypeStruct((1, WIDTH), jnp.float32)
    return pl.pallas_call(
        contrast_kernel,
        out_shape=(jax.ShapeDtypeStruct((1, 1), jnp.float32), row, row),
        in_specs=[SMEM, SMEM] + [VMEM] * 10,
        out_specs=(VMEM, VMEM, VMEM),
        scratch_shapes=[pltpu.VMEM((PAIRS, WIDTH), jnp.float32)] * 2,
        compiler_params=pltpu.CompilerParams(vmem_limit_bytes=32 * 2**20),
        name="contrast",
    )(places, scale, *blocks, *other_blocks)


def expert_kernel(rows_ref, in_own, in_other, out_own, out_other, out_ref, hidden_scr):
    rows = rows_ref[...]
    share = in_own.shape[1]
    tile = 2 * LANES
    whole = share // tile * tile
    cuts = [slice(i, i + tile) for i in range(0, whole, tile)]

    def hidden_of(first):
        hidden = jax.nn.gelu(jnp.dot(rows, first, preferred_element_type=jnp.float32))
        return narrow(hidden)

    for cut in cuts:
        hidden_scr[:, cut] = hidden_of(in_own[:, cut])
        hidden_scr[:, share + cut.start : share + cut.stop] = hidden_of(in_other[:, cut])
    last = hidden_of(jnp.concatenate([in_own[:, whole:], in_other[:, whole:]], axis=1))
    hidden_scr[:, whole:share] = last[:, : share - whole]
    hidden_scr[:, share + whole :] = last[:, share - whole :]
    hidden = hidden_scr[...]
    for i in range(0, out_ref.shape[1], tile):
        cut = slice(i, i + tile)
        second = jnp.concatenate([out_own[:, cut], out_other[:, cut]], axis=0)
        out_ref[:, cut] = jnp.dot(hidden, second, preferred_element_type=jnp.float32)


def expert_rows(rows, in_own, in_other, out_own, out_other):
    count, width = rows.shape
    hidden = in_own.shape[1]
    return pl.pallas_call(
        expert_kernel,
        out_shape=jax.ShapeDtypeStruct((count, width), jnp.float32),
        in_specs=[VMEM] * 5,
        out_specs=VMEM,
        scratch_shapes=[pltpu.VMEM((count, 2 * hidden), jnp.bfloat16)],
        compiler_params=pltpu.CompilerParams(vmem_limit_bytes=32 * 2**20),
        cost_estimate=pl.CostEstimate(
            flops=8 * count * width * hidden,
            bytes_accessed=8 * width * hidden + 6 * count * width,
            transcendentals=2 * count * hidden,
        ),
        name="expert",
    )(rows, in_own, in_other, out_own, out_other)


def along_x(step):
    return "dp", [(x * 2 + c, (x + step) % X * 2 + c) for x in range(X) for c in range(CORES)]


def along_core():
    return "dp", [(i, i ^ 1) for i in range(X * CORES)]


def to_experts(blocks):
    return lax.all_to_all(blocks, "expert", split_axis=0, concat_axis=0, tiled=True)


def on_device(
    tokens, norm_gain, expert_ids, priority, gate_prob, w_in, w_out, text_emb, logit_scale
):
    rows, width = tokens.shape
    half = SLOTS // 2
    dp_place = lax.axis_index("dp")
    places = jnp.stack([dp_place // CORES, dp_place % CORES, lax.axis_index("expert")])

    key = expert_ids.reshape(1, rows) * 256 + priority
    outgoing, target = dispatch(tokens, norm_gain.reshape(width // LANES, LANES), key)

    weights = (
        w_in[0],
        lax.ppermute(w_in[0], *along_core()),
        w_out[0],
        lax.ppermute(w_out[0], *along_core()),
    )

    own_rows = to_experts(outgoing.reshape(Y * Z, CAP, width)).reshape(SLOTS, width)

    left_rows = lax.ppermute(own_rows, *along_x(1))
    right_rows = lax.ppermute(own_rows, *along_x(-1))
    own_part = expert_rows(own_rows, *weights)
    left_rows, right_rows, own_part = lax.optimization_barrier((left_rows, right_rows, own_part))
    far_rows = jnp.concatenate(
        [
            lax.ppermute(left_rows[:half], *along_x(1)),
            lax.ppermute(right_rows[half:], *along_x(-1)),
        ]
    )
    side_part = expert_rows(jnp.concatenate([left_rows, right_rows]), *weights)
    far_rows, side_part = lax.optimization_barrier((far_rows, side_part))
    far_part = narrow(expert_rows(far_rows, *weights))

    from_right = lax.ppermute(far_part[:half], *along_x(-1))
    from_left = lax.ppermute(far_part[half:], *along_x(1))
    left_sum = jnp.concatenate([side_part[:half] + wide(from_right), side_part[half:SLOTS]])
    right_sum = jnp.concatenate(
        [side_part[SLOTS : SLOTS + half], side_part[SLOTS + half :] + wide(from_left)]
    )
    left_sum = lax.ppermute(narrow(left_sum), *along_x(-1))
    right_sum = lax.ppermute(narrow(right_sum), *along_x(1))
    result = narrow(own_part + wide(left_sum) + wide(right_sum))

    returned = to_experts(result.reshape(Y * Z, CAP, width)).reshape(SLOTS, width)
    moe_out, pair = combine(returned, target, gate_prob.reshape(1, rows), tokens, text_emb)

    near = to_experts(pair.reshape(Y * Z, 1, 2 * width)).reshape(pair.shape)
    half = near.shape[0] // 2
    left = lax.ppermute(near, *along_x(1))
    right = lax.ppermute(near, *along_x(-1))
    far = [lax.ppermute(left[:half], *along_x(1)), lax.ppermute(right[half:], *along_x(-1))]
    blocks = [near, left, right] + far
    loss, grad_image, grad_text = contrast(
        places,
        logit_scale,
        blocks,
        [lax.ppermute(block, *along_core()) for block in blocks],
    )
    return (moe_out, loss.reshape(1), grad_image, grad_text)


def solution(mesh):
    in_specs = (
        P(("dp", "expert"), None),
        P(),
        P(("dp", "expert"), None),
        P(("dp", "expert"), None),
        P(("dp", "expert")),
        P("expert", None, "dp"),
        P("expert", "dp", None),
        P(("dp", "expert"), None),
        P(),
    )
    out_specs = (
        P(("dp", "expert"), None),
        P(),
        P(("dp", "expert"), None),
        P(("dp", "expert"), None),
    )
    return jax.shard_map(
        on_device, mesh=mesh, in_specs=in_specs, out_specs=out_specs, check_vma=False
    )
```

```python
import jax
import jax.numpy as jnp
from jax import lax
from jax.experimental import pallas as pl
from jax.experimental.pallas import tpu as pltpu
from jax.sharding import PartitionSpec as P

X, CORES, Y, Z = 4, 2, 4, 8
CAP = 4
LANES, WIDTH = 128, 1280
SLOTS = Y * Z * CAP
PAIRS = X * CORES * Y * Z
VMEM = pl.BlockSpec(memory_space=pltpu.VMEM)
SMEM = pl.BlockSpec(memory_space=pltpu.SMEM)


def narrow(values):
    return values.astype(jnp.bfloat16)


def wide(values):
    return values.astype(jnp.float32)


def iota(shape, dim):
    return lax.broadcasted_iota(jnp.int32, shape, dim)


def as_column(row):
    n = row.shape[1]
    same = iota((n, n), 0) == iota((n, n), 1)
    return jnp.sum(jnp.where(same, row, 0.0), axis=1, keepdims=True)


def table_of(target):
    return narrow(wide(iota((SLOTS, target.shape[1]), 0) == target))


def dispatch_kernel(tokens_ref, gain_ref, key_ref, out_ref, target_ref):
    whole_key = key_ref[...]
    ids = whole_key >> 8
    base, key = wide(ids * 256), wide(whole_key)
    others = as_column(key)
    earlier = (others >= base) & (others < key)
    slots = jnp.sum(wide(earlier), axis=0, keepdims=True).astype(jnp.int32)
    target = jnp.where(slots < CAP, ids * CAP + slots, -1)
    target_ref[...] = target
    values = wide(tokens_ref[...])
    center = values - jnp.mean(values, axis=-1, keepdims=True)
    spread = jnp.mean(center * center, axis=-1, keepdims=True)
    gain = jnp.concatenate([gain_ref[i : i + 1, :] for i in range(gain_ref.shape[0])], axis=1)
    normed = narrow(center * lax.rsqrt(spread + 1e-06) * gain)
    out_ref[...] = narrow(
        jnp.dot(table_of(target), normed, preferred_element_type=jnp.float32)
    )


def dispatch(tokens, gain, key):
    rows, width = tokens.shape
    return pl.pallas_call(
        dispatch_kernel,
        out_shape=(
            jax.ShapeDtypeStruct((SLOTS, width), jnp.bfloat16),
            jax.ShapeDtypeStruct((1, rows), jnp.int32),
        ),
        in_specs=[VMEM] * 3,
        out_specs=(VMEM, VMEM),
        compiler_params=pltpu.CompilerParams(vmem_limit_bytes=24 * 2**20),
        name="dispatch",
    )(tokens, gain, key)


def combine_kernel(
    returned_ref, target_ref, gate_ref, tokens_ref, text_ref, out_ref, pair_ref
):
    expert_part = lax.dot_general(
        table_of(target_ref[...]),
        returned_ref[...],
        (((0,), (0,)), ((), ())),
        preferred_element_type=jnp.float32,
    )
    moe_out = narrow(wide(tokens_ref[...]) + as_column(gate_ref[...]) * expert_part)
    out_ref[...] = moe_out
    pooled = jnp.mean(wide(moe_out), axis=0, keepdims=True)
    pair = jnp.concatenate([pooled, text_ref[...]], axis=1)
    pieces = pair.shape[1] // LANES
    for index in range(pieces):
        piece = pair[:, index * LANES : (index + 1) * LANES]
        pair_ref[pl.ds(index, Y * Z, stride=pieces), :] = jnp.broadcast_to(piece, (Y * Z, LANES))


def combine(returned, target, gate, tokens, text):
    rows, width = tokens.shape
    return pl.pallas_call(
        combine_kernel,
        out_shape=(
            jax.ShapeDtypeStruct((rows, width), jnp.bfloat16),
            jax.ShapeDtypeStruct((Y * Z * 2 * width // LANES, LANES), jnp.float32),
        ),
        in_specs=[VMEM] * 5,
        out_specs=(VMEM, VMEM),
        compiler_params=pltpu.CompilerParams(vmem_limit_bytes=24 * 2**20),
        name="combine",
    )(returned, target, gate, tokens, text)


def full_rows(ref, which):
    pieces = WIDTH // LANES
    count = ref.shape[0] // (2 * pieces)
    return jnp.concatenate(
        [ref[pl.ds(which * pieces + i, count, stride=2 * pieces), :] for i in range(pieces)],
        axis=1,
    )


def contrast_kernel(place_ref, scale_ref, *refs):
    blocks = (refs[:5], refs[5:10])
    loss_ref, image_ref, dtext_ref, image_scr, text_scr = refs[10:]
    place_x, core, expert = place_ref[0], place_ref[1], place_ref[2]
    me = (place_x * CORES + core) * (Y * Z) + expert
    scale = scale_ref[0]

    half = Y * Z // 2
    for side in range(CORES):
        c = core + side - 2 * core * side
        for ref, step, first in zip(blocks[side], (0, 3, 1, 2, 2), (0, 0, 0, 0, half)):
            x = (place_x + step) & (X - 1)
            start = pl.multiple_of((x * CORES + c) * (Y * Z) + first, 8)
            for which, scratch in enumerate((image_scr, text_scr)):
                rows = full_rows(ref, which)
                square = jnp.sum(rows * rows, axis=-1, keepdims=True)
                scratch[pl.ds(start, rows.shape[0]), :] = rows / jnp.sqrt(square + 1e-06)
    image_unit = image_scr[...]
    text_unit = text_scr[...]
    logits = scale * lax.dot_general(
        image_unit,
        text_unit,
        (((1,), (1,)), ((), ())),
        precision=lax.Precision.HIGHEST,
        preferred_element_type=jnp.float32,
    )
    row_max = jnp.max(logits, axis=1, keepdims=True)
    col_max = jnp.max(logits, axis=0, keepdims=True)
    row_lse = row_max + jnp.log(jnp.sum(jnp.exp(logits - row_max), axis=1, keepdims=True))
    col_lse = col_max + jnp.log(jnp.sum(jnp.exp(logits - col_max), axis=0, keepdims=True))
    rows_at, cols_at = iota(logits.shape, 0), iota(logits.shape, 1)
    same = rows_at == cols_at
    trace = jnp.sum(jnp.where(same, logits, 0.0), axis=(0, 1), keepdims=True)
    total = jnp.sum(row_lse, axis=0, keepdims=True) + jnp.sum(col_lse, axis=1, keepdims=True)
    loss_ref[...] = (total - 2.0 * trace) / (2.0 * PAIRS)
    grad = jnp.exp(logits - row_lse) + jnp.exp(logits - col_lse) - 2.0 * wide(same)
    grad = grad / (2.0 * PAIRS)
    own_col = jnp.sum(jnp.where(cols_at == me, grad, 0.0), axis=1, keepdims=True)
    own_row = as_column(jnp.sum(jnp.where(rows_at == me, grad, 0.0), axis=0, keepdims=True))
    d_image = scale * jnp.sum(own_row * text_unit, axis=0, keepdims=True)
    d_text = scale * jnp.sum(own_col * image_unit, axis=0, keepdims=True)

    def back(unit, radius, upstream):
        along = jnp.sum(unit * upstream, axis=-1, keepdims=True)
        return (upstream - unit * along) / radius

    def own(rows):
        radius = jnp.sqrt(jnp.sum(rows * rows, axis=-1, keepdims=True) + 1e-06)
        return rows / radius, radius

    def own_row(which):
        pieces = WIDTH // LANES
        first = (2 * expert + which) * pieces
        return jnp.concatenate(
            [blocks[0][0][pl.ds(first + i, 1), :] for i in range(pieces)], axis=1
        )

    image_ref[...] = back(*own(own_row(0)), d_image)
    dtext_ref[...] = back(*own(own_row(1)), d_text)


def contrast(places, scale, blocks, other_blocks):
    row = jax.ShapeDtypeStruct((1, WIDTH), jnp.float32)
    return pl.pallas_call(
        contrast_kernel,
        out_shape=(jax.ShapeDtypeStruct((1, 1), jnp.float32), row, row),
        in_specs=[SMEM, SMEM] + [VMEM] * 10,
        out_specs=(VMEM, VMEM, VMEM),
        scratch_shapes=[pltpu.VMEM((PAIRS, WIDTH), jnp.float32)] * 2,
        compiler_params=pltpu.CompilerParams(vmem_limit_bytes=32 * 2**20),
        name="contrast",
    )(places, scale, *blocks, *other_blocks)


def expert_kernel(rows_ref, in_own, in_other, out_own, out_other, out_ref, hidden_scr):
    rows = rows_ref[...]
    share = in_own.shape[1]
    tile = 2 * LANES
    whole = share // tile * tile
    cuts = [slice(i, i + tile) for i in range(0, whole, tile)]

    def hidden_of(first):
        hidden = jax.nn.gelu(jnp.dot(rows, first, preferred_element_type=jnp.float32))
        return narrow(hidden)

    for cut in cuts:
        hidden_scr[:, cut] = hidden_of(in_own[:, cut])
        hidden_scr[:, share + cut.start : share + cut.stop] = hidden_of(in_other[:, cut])
    last = hidden_of(jnp.concatenate([in_own[:, whole:], in_other[:, whole:]], axis=1))
    hidden_scr[:, whole:share] = last[:, : share - whole]
    hidden_scr[:, share + whole :] = last[:, share - whole :]
    hidden = hidden_scr[...]
    for i in range(0, out_ref.shape[1], tile):
        cut = slice(i, i + tile)
        second = jnp.concatenate([out_own[:, cut], out_other[:, cut]], axis=0)
        out_ref[:, cut] = jnp.dot(hidden, second, preferred_element_type=jnp.float32)


def expert_rows(rows, in_own, in_other, out_own, out_other):
    count, width = rows.shape
    hidden = in_own.shape[1]
    return pl.pallas_call(
        expert_kernel,
        out_shape=jax.ShapeDtypeStruct((count, width), jnp.float32),
        in_specs=[VMEM] * 5,
        out_specs=VMEM,
        scratch_shapes=[pltpu.VMEM((count, 2 * hidden), jnp.bfloat16)],
        compiler_params=pltpu.CompilerParams(vmem_limit_bytes=32 * 2**20),
        cost_estimate=pl.CostEstimate(
            flops=8 * count * width * hidden,
            bytes_accessed=8 * width * hidden + 6 * count * width,
            transcendentals=2 * count * hidden,
        ),
        name="expert",
    )(rows, in_own, in_other, out_own, out_other)


def along_x(step):
    return "dp", [(x * 2 + c, (x + step) % X * 2 + c) for x in range(X) for c in range(CORES)]


def along_core():
    return "dp", [(i, i ^ 1) for i in range(X * CORES)]


def to_experts(blocks):
    return lax.all_to_all(blocks, "expert", split_axis=0, concat_axis=0, tiled=True)


def on_device(
    tokens, norm_gain, expert_ids, priority, gate_prob, w_in, w_out, text_emb, logit_scale
):
    rows, width = tokens.shape
    half = SLOTS // 2
    dp_place = lax.axis_index("dp")
    places = jnp.stack([dp_place // CORES, dp_place % CORES, lax.axis_index("expert")])

    key = expert_ids.reshape(1, rows) * 256 + priority
    outgoing, target = dispatch(tokens, norm_gain.reshape(width // LANES, LANES), key)

    own_rows = to_experts(outgoing.reshape(Y * Z, CAP, width)).reshape(SLOTS, width)

    own_rows, w_in, w_out = lax.optimization_barrier((own_rows, w_in, w_out))
    weights = (
        w_in[0],
        lax.ppermute(w_in[0], *along_core()),
        w_out[0],
        lax.ppermute(w_out[0], *along_core()),
    )

    left_rows = lax.ppermute(own_rows, *along_x(1))
    right_rows = lax.ppermute(own_rows, *along_x(-1))
    own_part = expert_rows(own_rows, *weights)
    left_rows, right_rows, own_part = lax.optimization_barrier((left_rows, right_rows, own_part))
    far_rows = jnp.concatenate(
        [
            lax.ppermute(left_rows[:half], *along_x(1)),
            lax.ppermute(right_rows[half:], *along_x(-1)),
        ]
    )
    side_part = expert_rows(jnp.concatenate([left_rows, right_rows]), *weights)
    far_rows, side_part = lax.optimization_barrier((far_rows, side_part))
    far_part = narrow(expert_rows(far_rows, *weights))

    from_right = lax.ppermute(far_part[:half], *along_x(-1))
    from_left = lax.ppermute(far_part[half:], *along_x(1))
    left_sum = jnp.concatenate([side_part[:half] + wide(from_right), side_part[half:SLOTS]])
    right_sum = jnp.concatenate(
        [side_part[SLOTS : SLOTS + half], side_part[SLOTS + half :] + wide(from_left)]
    )
    left_sum = lax.ppermute(narrow(left_sum), *along_x(-1))
    right_sum = lax.ppermute(narrow(right_sum), *along_x(1))
    result = narrow(own_part + wide(left_sum) + wide(right_sum))

    returned = to_experts(result.reshape(Y * Z, CAP, width)).reshape(SLOTS, width)
    moe_out, pair = combine(returned, target, gate_prob.reshape(1, rows), tokens, text_emb)

    near = to_experts(pair.reshape(Y * Z, 1, 2 * width)).reshape(pair.shape)
    half = near.shape[0] // 2
    left = lax.ppermute(near, *along_x(1))
    right = lax.ppermute(near, *along_x(-1))
    far = [lax.ppermute(left[:half], *along_x(1)), lax.ppermute(right[half:], *along_x(-1))]
    blocks = [near, left, right] + far
    loss, grad_image, grad_text = contrast(
        places,
        logit_scale,
        blocks,
        [lax.ppermute(block, *along_core()) for block in blocks],
    )
    return (moe_out, loss.reshape(1), grad_image, grad_text)


def solution(mesh):
    in_specs = (
        P(("dp", "expert"), None),
        P(),
        P(("dp", "expert"), None),
        P(("dp", "expert"), None),
        P(("dp", "expert")),
        P("expert", None, "dp"),
        P("expert", "dp", None),
        P(("dp", "expert"), None),
        P(),
    )
    out_specs = (
        P(("dp", "expert"), None),
        P(),
        P(("dp", "expert"), None),
        P(("dp", "expert"), None),
    )
    return jax.shard_map(
        on_device, mesh=mesh, in_specs=in_specs, out_specs=out_specs, check_vma=False
    )
```
